512 devices in a mesh: section: 16 (over z_hi, x, core), replica: 32 (over z_lo, y).
Axes of the slice: x: 4, y: 8, z: 8 (z_hi: 2, z_lo: 4; z = z_hi * 4 + z_lo), core: 2. Of those that a mesh axis runs over, the one named last changes fastest.
Arguments:
- codes_in: bfloat16 [16384, 384], P('replica'), may hold values from -6 to 6
- cotangent: bfloat16 [16384, 384], P('replica'), may hold values from -0.125 to 0.125
- up: bfloat16 [16, 384, 2560], P('section', None, 'replica'), may hold values from -0.3125 to 0.3125
- down: bfloat16 [16, 384, 2560], P('section', None, 'replica'), may hold values from -0.125 to 0.125
- gain: bfloat16 [16, 2560], P('section', 'replica'), may hold values from 0.099609375 to 1.8984375
Outputs:
- section_codes: bfloat16 [16, 16384, 384], P('section', 'replica')
- grad_up: float32 [16, 384, 2560], P('section', None, 'replica')
- grad_down: float32 [16, 384, 2560], P('section', None, 'replica')
- grad_gain: float32 [16, 2560], P('section', 'replica')
The draws below stay inside these ranges and needn't reach their ends.
All inputs are finite; a program needn't handle non-finite values.
Results may differ from the reference program's by a relative error of at most 0.04.
Values may be sent and summed in bfloat16 or wider, within the bound.
A program may use at most 64 MiB of HBM per device.

```python
import jax
import jax.numpy as jnp
from jax import lax

D = 2560
C = 384
TOK_DEV = 512
SECTIONS = 16
TOKENS = 16384
N_REPLICA = 32


def levels(key, shape, pieces, smallest, high):
    level = 1.0
    for position, blocks in pieces:
        draws = jax.random.uniform(jax.random.fold_in(jax.random.fold_in(key, 6), position), (blocks,), jnp.float32, smallest / len(pieces), high / len(pieces))
        level = level * jnp.repeat(jnp.exp(draws), shape[position] // blocks).reshape((-1,) + (1,) * (len(shape) - 1 - position))
    return level


def noise(rng, shape, scale, reach, pieces=(), held_as=jnp.bfloat16):
    entries = scale * jax.random.normal(rng, shape, jnp.float32)
    if pieces:
        entries = entries * levels(rng, shape, pieces, -0.22, 0.18)
    return jnp.clip(entries, -reach, reach).astype(held_as)


def setup_inputs(seed: int = 0) -> dict:
    seeds = jax.random.split(jax.random.key(seed), 6)
    return {
        "codes_in": noise(seeds[0], (TOKENS, C), 1.0, 6.0, ((0, 32),)),
        "cotangent": noise(seeds[1], (TOKENS, C), 0.0078125, 0.125, ((0, 32),)),
        "up": noise(seeds[2], (SECTIONS, C, D), C ** -0.5, 0.3125, ((0, 16), (2, 32))),
        "down": noise(seeds[3], (SECTIONS, C, D), D ** -0.5, 0.125, ((0, 16), (2, 32))),
        "gain": jnp.clip(1.0 + 0.18 * jax.random.normal(seeds[4], (SECTIONS, D), jnp.float32), 0.099609375, 1.8984375).astype(jnp.bfloat16),
    }


EPS = 1e-06

def forward_pieces(source, up_w, down_w, gain_f):
    hidden = jnp.dot(source, up_w, preferred_element_type=jnp.float32)
    scale = lax.rsqrt(lax.optimization_barrier(jnp.mean(hidden * hidden, axis=-1, keepdims=True)) + EPS)
    normed = hidden * scale * gain_f
    act = jax.nn.gelu(normed).astype(jnp.bfloat16)
    mixed = lax.dot_general(act, down_w, (((1,), (1,)), ((), ())), preferred_element_type=jnp.float32)
    result = (source.astype(jnp.float32) + mixed).astype(jnp.bfloat16)
    return (hidden, act, result)

def backward_pieces(hidden, g_out, up_w, down_w, gain_f):
    scale = lax.rsqrt(lax.optimization_barrier(jnp.mean(hidden * hidden, axis=-1, keepdims=True)) + EPS)
    normed = hidden * scale * gain_f
    d_act = jnp.dot(g_out, down_w, preferred_element_type=jnp.float32)
    d_norm = jax.vjp(jax.nn.gelu, normed)[1](d_act)[0]
    weighted = d_norm * gain_f
    gain_rows = d_norm * hidden * scale
    d_hid = (scale * (weighted - hidden * (scale * scale) * lax.optimization_barrier(jnp.mean(weighted * hidden, axis=-1, keepdims=True)))).astype(jnp.bfloat16)
    mixed = lax.dot_general(d_hid, up_w, (((1,), (1,)), ((), ())), preferred_element_type=jnp.float32)
    g_in = (g_out.astype(jnp.float32) + mixed).astype(jnp.bfloat16)
    return (d_hid, g_in, gain_rows)

def replica_sum(left, right):
    left_f = left.reshape(N_REPLICA, TOK_DEV, left.shape[-1]).astype(jnp.float32)
    right_f = right.reshape(N_REPLICA, TOK_DEV, right.shape[-1]).astype(jnp.float32)
    parts = jnp.einsum('rtc,rtd->rcd', left_f, right_f)
    return lax.optimization_barrier(jnp.sum(parts.astype(jnp.bfloat16).astype(jnp.float32), axis=0))

def reference(codes_in, cotangent, up, down, gain):

    def forward_section(codes, weights):
        up_w, down_w, gain_w = weights
        hidden, act, result = forward_pieces(codes, up_w, down_w, gain_w.astype(jnp.float32))
        return (result, (codes, result))
    _, (inputs, section_codes) = lax.scan(forward_section, codes_in, (up, down, gain))

    def backward_section(g_out, weights):
        up_w, down_w, gain_w, source = weights
        gain_f = gain_w.astype(jnp.float32)
        hidden, act, result = forward_pieces(source, up_w, down_w, gain_f)
        d_hid, g_in, gain_rows = backward_pieces(hidden, g_out, up_w, down_w, gain_f)
        grad_u = replica_sum(source, d_hid)
        grad_d = replica_sum(g_out, act)
        gain_parts = lax.optimization_barrier(jnp.sum(gain_rows.reshape(N_REPLICA, TOK_DEV, D), axis=1))
        grad_g = lax.optimization_barrier(jnp.sum(gain_parts.astype(jnp.bfloat16).astype(jnp.float32), axis=0))
        return (g_in, (grad_u, grad_d, grad_g))
    _, (grad_up, grad_down, grad_gain) = lax.scan(backward_section, cotangent, (up, down, gain, inputs), reverse=True)
    return (section_codes, grad_up, grad_down, grad_gain)
```

```python
import functools

import jax
import jax.numpy as jnp
from jax import lax
from jax.experimental import pallas as pl
from jax.experimental.pallas import tpu as pltpu
from jax.sharding import PartitionSpec as P

MESH = pl.DeviceIdType.MESH
EPS = 1e-06
NY, NZ = 8, 4
ROWS = 64
SPLIT = (48, 64)
C0 = 0.7978845608028654
C1 = 0.044715
NN = (((1,), (0,)), ((), ()))
TN = (((0,), (0,)), ((), ()))
F32 = jnp.float32
BF16 = jnp.bfloat16


def matmul(a, b, dims=NN):
    return lax.dot_general(a, b, dims, preferred_element_type=F32)


def kernel(
    codes, cot, up_in, dn_in, gain_in,
    codes_out, gu_out, gd_out, gg_out,
    up_t, dn_t, up_n, dn_n, gain_row,
    xb, gb, gi, act, wh, q, xs, sc, kk, h2,
    part_up, part_dn, rz_up, rz_dn, ry_up, ry_dn, rz2_up, rz2_dn, ry2_up, ry2_dn,
    gain_tot, gain_y, gain_z, gg_acc, gg_tot, gg_y, gg_z,
    zp1, yp1, zp2, yp2, gys, gzs, fx, bg, rz1, ry1, rz2, ry2, hys, hzs,
):
    last = lax.axis_size("section") - 1
    s = lax.axis_index("section")
    r = lax.axis_index("replica")
    y = lax.rem(r, NY)
    z = r // NY
    micro = xb.shape[0]
    feat = gain_row.shape[1]
    lanes = feat // 128
    width = xb.shape[2]

    def at_y(d):
        return lax.rem(y + d + NY, NY)

    def at_z(d):
        return lax.rem(z + d + NZ, NZ)

    def dev(z_, y_):
        return (s, z_ * NY + y_)

    pending = []

    def copy(src, dst, sems, index, to):
        return pltpu.make_async_remote_copy(
            src_ref=src, dst_ref=dst,
            send_sem=sems.at[(0,) + index], recv_sem=sems.at[(1,) + index],
            device_id=to, device_id_type=MESH,
        )

    def send(src, dst, sems, index, to, cond=None):
        c = copy(src, dst, sems, index, to)
        if cond is None:
            c.start()
        else:
            pl.when(cond)(c.start)
        pending.append((c, cond))

    def arrived(dst, sems, index, cond=None):
        c = copy(dst, dst, sems, index, (s, r))
        if cond is None:
            c.wait_recv()
        else:
            pl.when(cond)(c.wait_recv)

    barrier = pltpu.get_barrier_semaphore()
    for d in range(1, NY):
        pl.semaphore_signal(barrier, inc=1, device_id=dev(z, at_y(d)), device_id_type=MESH)
    for d in range(1, NZ):
        pl.semaphore_signal(barrier, inc=1, device_id=dev(at_z(d), y), device_id_type=MESH)

    @pl.when(s > 0)
    def _():
        pl.semaphore_signal(barrier, inc=1, device_id=(s - 1, r), device_id_type=MESH)

    @pl.when(s < last)
    def _():
        pl.semaphore_signal(barrier, inc=1, device_id=(s + 1, r), device_id_type=MESH)

    pl.semaphore_wait(
        barrier, NY - 1 + NZ - 1 + jnp.where(s > 0, 1, 0) + jnp.where(s < last, 1, 0)
    )

    full = (up_t, dn_t)
    own = (up_in, dn_in)
    for a in range(2):
        kz = SPLIT[a]
        for d in range(1, NZ):
            send(own[a].at[0:kz], full[a].at[z, y, 0:kz], zp1, (a, d), dev(at_z(d), y))
        for d in range(1, NY):
            send(own[a].at[kz:], full[a].at[z, y, kz:], yp1, (a, d), dev(z, at_y(d)))
    for d in range(1, NY):
        send(gain_in, gain_y.at[d], gys, (d,), dev(z, at_y(d)))
    for a in range(2):
        full[a][z, y] = own[a][...]

    @pl.when(s == 0)
    def _():
        xb[...] = codes[...].reshape(xb.shape)

    @pl.when(s == last)
    def _():
        gb[...] = cot[...].reshape(gb.shape)

    def block_y(a, d):
        return full[a].at[:, at_y(d), 0:SPLIT[a]]

    def half_y(a, d, side):
        return full[a].at[2 * side:2 * side + 2, at_y(d), 0:SPLIT[a]]

    def block_z(a, i):
        return full[a].at[i, :, SPLIT[a]:]

    right, left = dev(z, at_y(1)), dev(z, at_y(-1))
    above, below = dev(jnp.minimum(z + 1, NZ - 1), y), dev(jnp.maximum(z - 1, 0), y)
    for a in range(2):
        for d in range(1, NZ):
            arrived(full[a].at[at_z(-d), y, 0:SPLIT[a]], zp1, (a, d))
        send(block_y(a, 0), block_y(a, 0), zp2, (a, 0, 0), right)
        send(block_y(a, 0), block_y(a, 0), zp2, (a, 1, 0), left)
    for a in range(2):
        for d in range(1, NY):
            arrived(full[a].at[z, at_y(-d), SPLIT[a]:], yp1, (a, d))
        send(block_z(a, z), block_z(a, z), yp2, (a, 0, 0), above, z < NZ - 1)
        send(block_z(a, z), block_z(a, z), yp2, (a, 1, 0), below, z > 0)
    total = gain_in[...]
    for d in range(1, NY):
        arrived(gain_y.at[d], gys, (d,))
        total = total + gain_y[d]
    gain_tot[...] = total
    for d in range(1, NZ):
        send(gain_tot, gain_z.at[d], gzs, (d,), dev(at_z(d), y))
    for k in range(1, 4):
        for a in range(2):
            arrived(block_y(a, -k), zp2, (a, 0, k - 1))
            if k < 3:
                send(block_y(a, -k), block_y(a, -k), zp2, (a, 0, k), right)
            else:
                send(half_y(a, -k, 0), half_y(a, -k, 0), zp2, (a, 0, k), right)
            arrived(block_y(a, k), zp2, (a, 1, k - 1))
            if k < 3:
                send(block_y(a, k), block_y(a, k), zp2, (a, 1, k), left)
            else:
                send(half_y(a, k, 1), half_y(a, k, 1), zp2, (a, 1, k), left)
        for a in range(2):
            up_block, dn_block = block_z(a, jnp.maximum(z - k, 0)), block_z(a, jnp.minimum(z + k, NZ - 1))
            arrived(up_block, yp2, (a, 0, k - 1), z >= k)
            if k < 3:
                send(up_block, up_block, yp2, (a, 0, k), above, (z >= k) & (z < NZ - 1))
            arrived(dn_block, yp2, (a, 1, k - 1), z <= NZ - 1 - k)
            if k < 3:
                send(dn_block, dn_block, yp2, (a, 1, k), below, (z <= NZ - 1 - k) & (z > 0))
    for a in range(2):
        arrived(half_y(a, -4, 0), zp2, (a, 0, 3))
        arrived(half_y(a, 4, 1), zp2, (a, 1, 3))
    total = gain_tot[...]
    for d in range(1, NZ):
        arrived(gain_z.at[d], gzs, (d,))
        total = total + gain_z[d]
    for c in range(lanes):
        gain_row[:, 128 * c:128 * (c + 1)] = total[c:c + 1, :]

    group = feat // NZ
    for i in range(NZ):
        up_n[:, group * i:group * (i + 1)] = up_t[i].reshape(group, width).T

    def forward(m, _):
        @pl.when(s > 0)
        def _():
            arrived(xb.at[m], fx, (m,))

        x = xb[m]
        hidden = matmul(x, up_n[...])
        scale = lax.rsqrt(jnp.sum(hidden * hidden, axis=1, keepdims=True) * (1.0 / feat) + EPS)
        v = hidden * scale * gain_row[...]
        t = jnp.tanh(C0 * (v + C1 * (v * v * v)))
        a = (0.5 * v * (1.0 + t)).astype(BF16)
        out = (x.astype(F32) + matmul(a, dn_t[...].reshape(feat, width))).astype(BF16)
        codes_out[m] = out

        @pl.when(s < last)
        def _():
            copy(codes_out.at[m], xb.at[m], fx, (m,), (s + 1, r)).start()

        act[m] = a
        wh[1, m] = hidden.astype(BF16)
        sc[m] = jnp.broadcast_to(scale, sc.shape[1:])
        return 0

    lax.fori_loop(0, micro, forward, 0)

    for i in range(NZ):
        dn_n[:, group * i:group * (i + 1)] = dn_t[i].reshape(group, width).T

    def prepare(m, _):
        h_b = wh[1, m]
        hidden = h_b.astype(F32)
        scale = sc[m][:, 0:1]
        gain = gain_row[...]
        v = hidden * scale * gain
        v2 = v * v
        t = jnp.tanh(C0 * v * (1.0 + C1 * v2))
        slope = 0.5 * (1.0 + t) + (0.5 * C0) * v * (1.0 - t * t) * (1.0 + (3.0 * C1) * v2)
        q_f = slope * gain
        q[m] = q_f.astype(BF16)
        kk[m] = matmul((q_f * hidden).astype(BF16), dn_t[...].reshape(feat, width)) * (1.0 / feat)
        h2[m] = matmul(h_b, up_t[...].reshape(feat, width)) * (scale * scale * scale)
        return 0

    lax.fori_loop(0, micro, prepare, 0)

    def backward(m, _):
        @pl.when(s < last)
        def _():
            arrived(gb.at[m], bg, (m,))

        g = gb[m]
        g_f = g.astype(F32)
        w = (matmul(g, dn_n[...]) * q[m].astype(F32)).astype(BF16)
        mean = jnp.sum(g_f * kk[m], axis=1, keepdims=True)
        scale = sc[m][:, 0:1]
        mixed = matmul(w, up_t[...].reshape(feat, width))
        gi[m] = (g_f + scale * mixed - mean * h2[m]).astype(BF16)

        @pl.when(s > 0)
        def _():
            copy(gi.at[m], gb.at[m], bg, (m,), (s - 1, r)).start()

        wh[0, m] = w
        x = xb[m].astype(F32)
        xs[0, m] = (scale * x).astype(BF16)
        xs[1, m] = (x * (-(scale * scale * scale) * mean)).astype(BF16)
        return 0

    lax.fori_loop(0, micro, backward, 0)

    parts = (part_up, part_dn)
    rz, ry, z2, y2 = (rz_up, rz_dn), (ry_up, ry_dn), (rz2_up, rz2_dn), (ry2_up, ry2_dn)
    outs = (gu_out, gd_out)

    def part_y(a, d):
        return parts[a].at[:, at_y(d), 0:SPLIT[a]]

    def part_z(a, i):
        return parts[a].at[i, :, SPLIT[a]:]

    def add_into(ref, other):
        ref[...] = (ref[...].astype(F32) + other[...].astype(F32)).astype(BF16)

    def first_sends(a):
        kz = SPLIT[a]
        send(parts[a].at[0:2, at_y(4), 0:kz], rz[a].at[0, 0, 0:2], rz1, (a, 0, 0), right)
        send(parts[a].at[2:4, at_y(4), 0:kz], rz[a].at[1, 0, 2:4], rz1, (a, 1, 0), left)
        send(part_z(a, NZ - 1), ry[a].at[0, NZ - 1], ry1, (a, 0, NZ - 1), above, z == 0)
        send(part_z(a, 0), ry[a].at[1, 0], ry1, (a, 1, 0), below, z == NZ - 1)

    rows = micro * ROWS
    for i in range(NZ):
        cols = slice(group * i, group * (i + 1))
        part_dn[i] = matmul(
            act[:, :, cols].reshape(rows, group), gb[...].reshape(rows, width), TN
        ).astype(BF16).reshape(part_dn.shape[1:])
    first_sends(1)
    for i in range(NZ):
        cols = slice(group * i, group * (i + 1))
        part_up[i] = matmul(
            wh[:, :, :, cols].reshape(2 * rows, group), xs[...].reshape(2 * rows, width), TN
        ).astype(BF16).reshape(part_up.shape[1:])
    first_sends(0)

    gg_acc[...] = jnp.zeros_like(gg_acc)

    def gain_rows(m, _):
        term = wh[0, m].astype(F32) * (wh[1, m].astype(F32) * sc[m][:, 0:1])
        gg_acc[...] += jnp.sum(term.reshape(ROWS // 8, 8, feat), axis=0)
        return 0

    lax.fori_loop(0, micro, gain_rows, 0)
    total = jnp.sum(gg_acc[...], axis=0, keepdims=True) / gain_row[...]
    gg_tot[0] = jnp.zeros_like(gg_tot[0])
    for c in range(lanes):
        gg_tot[0, c:c + 1, :] = total[:, 128 * c:128 * (c + 1)]
    for d in range(1, NY):
        send(gg_tot.at[0], gg_y.at[d], hys, (d,), dev(z, at_y(d)))

    for k in range(1, 4):
        for a in (1, 0):
            for side in range(2):
                sign = 1 - 2 * side
                to = (right, left)[side]
                if k == 1:
                    half = slice(2 * side, 2 * side + 2)
                    got = rz[a].at[side, 0, half]
                    arrived(got, rz1, (a, side, 0))
                    add_into(parts[a].at[half, at_y(3 * sign), 0:SPLIT[a]], got)
                else:
                    got = rz[a].at[side, k - 1]
                    arrived(got, rz1, (a, side, k - 1))
                    add_into(part_y(a, (4 - k) * sign), got)
                send(part_y(a, (4 - k) * sign), rz[a].at[side, k], rz1, (a, side, k), to)
        for a in (1, 0):
            for side in range(2):
                zt = (NZ - k, k - 1)[side]
                ahead = (z < zt, z > zt)[side]
                fed = ((z > 0) & (z <= zt), (z < NZ - 1) & (z >= zt))[side]
                to = (above, below)[side]
                got = ry[a].at[side, zt]

                @pl.when(fed)
                def _():
                    arrived(got, ry1, (a, side, zt))
                    add_into(part_z(a, zt), got)

                if k == 1:
                    sent_already = (z > 0, z < NZ - 1)[side]
                    c = copy(part_z(a, zt), got, ry1, (a, side, zt), to)
                    pl.when(ahead & sent_already)(c.start)
                    pending.append((c, ahead & sent_already))
                else:
                    send(part_z(a, zt), got, ry1, (a, side, zt), to, ahead)
        if k == 1:
            total = gg_tot[0]
            for d in range(1, NY):
                arrived(gg_y.at[d], hys, (d,))
                total = total + gg_y[d]
            gg_tot[1] = total
            for d in range(1, NZ):
                send(gg_tot.at[1], gg_z.at[d], hzs, (d,), dev(at_z(d), y))

    for a in (1, 0):
        kz = SPLIT[a]
        for d in range(1, NY):
            send(parts[a].at[z, at_y(d), kz:], y2[a].at[d], ry2, (a, d), dev(z, at_y(d)))
    for a in (1, 0):
        kz = SPLIT[a]
        for side in range(2):
            arrived(rz[a].at[side, 3], rz1, (a, side, 3))
        add = rz[a][0, 3].astype(F32) + rz[a][1, 3].astype(F32)
        mine = part_y(a, 0)
        mine[...] = (mine[...].astype(F32) + add).astype(BF16)
        for d in range(1, NZ):
            send(parts[a].at[at_z(d), y, 0:kz], z2[a].at[d], rz2, (a, d), dev(at_z(d), y))
    for a in (1, 0):
        kz = SPLIT[a]
        total = parts[a][z, y, kz:].astype(F32)
        for d in range(1, NY):
            arrived(y2[a].at[d], ry2, (a, d))
            total = total + y2[a][d].astype(F32)
        outs[a][kz:] = total
    for a in (1, 0):
        kz = SPLIT[a]
        total = parts[a][z, y, 0:kz].astype(F32)
        for d in range(1, NZ):
            arrived(z2[a].at[d], rz2, (a, d))
            total = total + z2[a][d].astype(F32)
        outs[a][0:kz] = total
    total = gg_tot[1]
    for d in range(1, NZ):
        arrived(gg_z.at[d], hzs, (d,))
        total = total + gg_z[d]
    gg_out[...] = total

    for c, cond in pending:
        if cond is None:
            c.wait_send()
        else:
            pl.when(cond)(c.wait_send)

    def drain(m, _):
        @pl.when(s < last)
        def _():
            copy(codes_out.at[m], xb.at[m], fx, (m,), (s + 1, r)).wait_send()

        @pl.when(s > 0)
        def _():
            copy(gi.at[m], gb.at[m], bg, (m,), (s - 1, r)).wait_send()

        return 0

    lax.fori_loop(0, micro, drain, 0)


def on_device(codes_in, cotangent, up, down, gain):
    rows, width = codes_in.shape
    piece = up.shape[2]
    feat = piece * lax.axis_size("replica")
    micro = rows // ROWS
    lanes = feat // 128
    pad = (-lanes) % 8
    offset = lax.axis_index("replica") * piece
    up_t = up[0].T
    dn_t = down[0].T
    gain_p = lax.dynamic_update_slice(
        jnp.zeros(((lanes + pad) * 128,), F32), gain[0].astype(F32), (offset,)
    ).reshape(lanes + pad, 128)
    grid = (NZ, NY, piece, width)
    small = (lanes + pad, 128)

    def vm(shape, dtype=BF16):
        return pltpu.VMEM(shape, dtype)

    def sem(*shape):
        return pltpu.SemaphoreType.DMA((2,) + shape)

    ku, kd = SPLIT
    scratch = [
        vm(grid), vm(grid), vm((width, feat)), vm((width, feat)), vm((1, feat), F32),
        vm((micro, ROWS, width)), vm((micro, ROWS, width)), vm((micro, ROWS, width)),
        vm((micro, ROWS, feat)), vm((2, micro, ROWS, feat)), vm((micro, ROWS, feat)),
        vm((2, micro, ROWS, width)), vm((micro, ROWS, 128), F32),
        vm((micro, ROWS, width), F32), vm((micro, ROWS, width), F32),
        vm(grid), vm(grid),
        vm((2, 4, NZ, ku, width)), vm((2, 4, NZ, kd, width)),
        vm((2, NZ, NY, piece - ku, width)), vm((2, NZ, NY, piece - kd, width)),
        vm((NZ, ku, width)), vm((NZ, kd, width)),
        vm((NY, piece - ku, width)), vm((NY, piece - kd, width)),
        vm(small, F32), vm((NY,) + small, F32), vm((NZ,) + small, F32),
        vm((8, feat), F32), vm((2,) + small, F32), vm((NY,) + small, F32), vm((NZ,) + small, F32),
        sem(2, NZ), sem(2, NY), sem(2, 2, 4), sem(2, 2, 3), sem(NY), sem(NZ),
        sem(micro), sem(micro),
        sem(2, 2, 4), sem(2, 2, NZ), sem(2, NZ), sem(2, NY), sem(NY), sem(NZ),
    ]
    codes, grad_up, grad_dn, grad_gain = pl.pallas_call(
        kernel,
        out_shape=(
            jax.ShapeDtypeStruct((micro, ROWS, width), BF16),
            jax.ShapeDtypeStruct((piece, width), F32),
            jax.ShapeDtypeStruct((piece, width), F32),
            jax.ShapeDtypeStruct(small, F32),
        ),
        in_specs=[pl.BlockSpec(memory_space=pltpu.VMEM)] * 5,
        out_specs=tuple([pl.BlockSpec(memory_space=pltpu.VMEM)] * 4),
        scratch_shapes=scratch,
        compiler_params=pltpu.CompilerParams(
            collective_id=0, has_side_effects=True, vmem_limit_bytes=56 << 20
        ),
    )(codes_in, cotangent, up_t, dn_t, gain_p)
    grad_gain = lax.dynamic_slice(grad_gain.reshape(-1), (offset,), (piece,))
    return (codes.reshape(1, rows, width), grad_up.T[None], grad_dn.T[None], grad_gain[None])


def solution(mesh):
    placed = (
        P("replica", None),
        P("replica", None),
        P("section", None, "replica"),
        P("section", None, "replica"),
        P("section", "replica"),
    )
    return jax.shard_map(
        on_device,
        mesh=mesh,
        in_specs=placed,
        out_specs=(
            P("section", "replica", None),
            P("section", None, "replica"),
            P("section", None, "replica"),
            P("section", "replica"),
        ),
        check_vma=False,
    )
```

```python
import functools

import jax
import jax.numpy as jnp
from jax import lax
from jax.experimental import pallas as pl
from jax.experimental.pallas import tpu as pltpu
from jax.sharding import PartitionSpec as P

MESH = pl.DeviceIdType.MESH
EPS = 1e-06
NY, NZ = 8, 4
ROWS = 64
SPLIT = (48, 64)
C0 = 0.7978845608028654
C1 = 0.044715
NN = (((1,), (0,)), ((), ()))
TN = (((0,), (0,)), ((), ()))
F32 = jnp.float32
BF16 = jnp.bfloat16


def matmul(a, b, dims=NN):
    return lax.dot_general(a, b, dims, preferred_element_type=F32)


def kernel(
    codes, cot, up_in, dn_in, gain_in,
    codes_out, gu_out, gd_out, gg_out,
    up_t, dn_t, up_n, dn_n, gain_row,
    xb, gb, gi, act, wh, q, xs, sc, kk, h2,
    part_up, part_dn, rz_up, rz_dn, ry_up, ry_dn, rz2_up, rz2_dn, ry2_up, ry2_dn,
    gain_tot, gain_y, gain_z, gg_acc, gg_tot, gg_y, gg_z, own,
    zp1, yp1, zp2, yp2, gys, gzs, fx, bg, rz1, ry1, rz2, ry2, hys, hzs,
):
    last = lax.axis_size("section") - 1
    s = lax.axis_index("section")
    r = lax.axis_index("replica")
    y = lax.rem(r, NY)
    z = r // NY
    micro = xb.shape[0]
    feat = gain_row.shape[1]
    width = xb.shape[2]

    def at_y(d):
        return lax.rem(y + d + NY, NY)

    def at_z(d):
        return lax.rem(z + d + NZ, NZ)

    def dev(z_, y_):
        return (s, z_ * NY + y_)

    pending = []

    def copy(src, dst, sems, index, to):
        return pltpu.make_async_remote_copy(
            src_ref=src, dst_ref=dst,
            send_sem=sems.at[(0,) + index], recv_sem=sems.at[(1,) + index],
            device_id=to, device_id_type=MESH,
        )

    def send(src, dst, sems, index, to, cond=None):
        c = copy(src, dst, sems, index, to)
        if cond is None:
            c.start()
        else:
            pl.when(cond)(c.start)
        pending.append((c, cond))

    def arrived(dst, sems, index, cond=None):
        c = copy(dst, dst, sems, index, (s, r))
        if cond is None:
            c.wait_recv()
        else:
            pl.when(cond)(c.wait_recv)

    barrier = pltpu.get_barrier_semaphore()
    for d in range(1, NY):
        pl.semaphore_signal(barrier, inc=1, device_id=dev(z, at_y(d)), device_id_type=MESH)
    for d in range(1, NZ):
        pl.semaphore_signal(barrier, inc=1, device_id=dev(at_z(d), y), device_id_type=MESH)

    @pl.when(s > 0)
    def _():
        pl.semaphore_signal(barrier, inc=1, device_id=(s - 1, r), device_id_type=MESH)

    @pl.when(s < last)
    def _():
        pl.semaphore_signal(barrier, inc=1, device_id=(s + 1, r), device_id_type=MESH)

    pl.semaphore_wait(
        barrier, NY - 1 + NZ - 1 + jnp.where(s > 0, 1, 0) + jnp.where(s < last, 1, 0)
    )

    full = (up_t, dn_t)
    for a in range(2):
        full[a][0, y] = (up_in, dn_in)[a][0].T

    def block_y(a, e, part=slice(0, NZ)):
        return full[a].at[part, at_y(e), 0:SPLIT[a]]

    def block_z(a, d):
        return full[a].at[d % NZ, :, SPLIT[a]:]

    right, left = dev(z, at_y(1)), dev(z, at_y(-1))
    above, below = dev(jnp.minimum(z + 1, NZ - 1), y), dev(jnp.maximum(z - 1, 0), y)
    first = (slice(0, 1), slice(0, 1))
    rest = (slice(1, NZ), slice(1, NZ))

    def ring(a, stream, side, k):
        if k < 3:
            return (first, rest)[stream][side]
        return ((slice(0, 1), None), (slice(1, 2), slice(2, NZ)))[stream][side]

    def ring_send(a, stream, side, k):
        part = ring(a, stream, side, k)
        if part is not None:
            e = (-k, k)[side]
            send(block_y(a, e, part), block_y(a, e, part), zp2, (a, stream, side, k), (right, left)[side])

    def ring_wait(a, stream, side, k):
        part = ring(a, stream, side, k)
        if part is not None:
            arrived(block_y(a, (-k - 1, k + 1)[side], part), zp2, (a, stream, side, k))

    for a in range(2):
        kz = SPLIT[a]
        for d in range(1, NZ):
            send(full[a].at[0, y, 0:kz], full[a].at[NZ - d, y, 0:kz], zp1, (a, d), dev(at_z(d), y))
        for d in range(1, NY):
            send(full[a].at[0, y, kz:], full[a].at[0, y, kz:], yp1, (a, d), dev(z, at_y(d)))
        for side in range(2):
            ring_send(a, 0, side, 0)
    for d in range(1, NY):
        send(gain_in, gain_y.at[d], gys, (d,), dev(z, at_y(d)))

    @pl.when(s == 0)
    def _():
        xb[...] = codes[...].reshape(xb.shape)

    @pl.when(s == last)
    def _():
        gb[...] = cot[...].reshape(gb.shape)

    for a in range(2):
        for d in range(1, NY):
            arrived(full[a].at[0, at_y(-d), SPLIT[a]:], yp1, (a, d))
        send(block_z(a, 0), block_z(a, -1), yp2, (a, 0, 0), above, z < NZ - 1)
        send(block_z(a, 0), block_z(a, 1), yp2, (a, 1, 0), below, z > 0)
        for d in range(1, NZ):
            arrived(full[a].at[NZ - d, y, 0:SPLIT[a]], zp1, (a, d))
        for side in range(2):
            ring_send(a, 1, side, 0)
    total = gain_in[...]
    for d in range(1, NY):
        arrived(gain_y.at[d], gys, (d,))
        total = total + gain_y[d]
    gain_tot[...] = total
    for d in range(1, NZ):
        send(gain_tot, gain_z.at[d], gzs, (d,), dev(at_z(d), y))
    for k in range(1, 4):
        for stream in range(2):
            for a in range(2):
                for side in range(2):
                    ring_wait(a, stream, side, k - 1)
                    ring_send(a, stream, side, k)
        for a in range(2):
            arrived(block_z(a, -k), yp2, (a, 0, k - 1), z >= k)
            if k < 3:
                send(block_z(a, -k), block_z(a, -k - 1), yp2, (a, 0, k), above, (z >= k) & (z < NZ - 1))
            arrived(block_z(a, k), yp2, (a, 1, k - 1), z <= NZ - 1 - k)
            if k < 3:
                send(block_z(a, k), block_z(a, k + 1), yp2, (a, 1, k), below, (z <= NZ - 1 - k) & (z > 0))
    for stream in range(2):
        for a in range(2):
            for side in range(2):
                ring_wait(a, stream, side, 3)
    total = gain_tot[...]
    for d in range(1, NZ):
        arrived(gain_z.at[d], gzs, (d,))
        total = total + gain_z[d]
    gain_z[0] = total
    group = feat // NZ
    for d in range(NZ):
        part = gain_z[0, at_z(d)]
        for c in range(group // 128):
            gain_row[:, group * d + 128 * c:group * d + 128 * (c + 1)] = part[c:c + 1, :]

    for i in range(NZ):
        up_n[:, group * i:group * (i + 1)] = up_t[i].reshape(group, width).T

    def forward(m, _):
        @pl.when(s > 0)
        def _():
            arrived(xb.at[m], fx, (m,))

        x = xb[m]
        hidden = matmul(x, up_n[...])
        scale = lax.rsqrt(jnp.sum(hidden * hidden, axis=1, keepdims=True) * (1.0 / feat) + EPS)
        v = hidden * scale * gain_row[...]
        t = jnp.tanh(C0 * (v + C1 * (v * v * v)))
        a = (0.5 * v * (1.0 + t)).astype(BF16)
        out = (x.astype(F32) + matmul(a, dn_t[...].reshape(feat, width))).astype(BF16)
        codes_out[m] = out

        @pl.when(s < last)
        def _():
            copy(codes_out.at[m], xb.at[m], fx, (m,), (s + 1, r)).start()

        slope = 0.5 * (1.0 + t) + (0.5 * C0) * v * (1.0 - t * t) * (1.0 + (3.0 * C1) * (v * v))
        q[m] = (slope * gain_row[...]).astype(BF16)
        act[m] = a
        wh[1, m] = hidden.astype(BF16)
        sc[m] = jnp.broadcast_to(scale, sc.shape[1:])
        return 0

    lax.fori_loop(0, micro, forward, 0)

    for i in range(NZ):
        dn_n[:, group * i:group * (i + 1)] = dn_t[i].reshape(group, width).T

    def prepare(i, _):
        some = pl.ds(i * (micro // 2), micro // 2)
        rows = micro // 2 * ROWS
        h_b = wh[1, some].reshape(rows, feat)
        product = q[some].reshape(rows, feat).astype(F32) * h_b.astype(F32)
        scale = sc[some].reshape(rows, 128)[:, 0:1]
        kk_f = matmul(product.astype(BF16), dn_t[...].reshape(feat, width)) * (1.0 / feat)
        kk[some] = kk_f.reshape(micro // 2, ROWS, width)
        h2_f = matmul(h_b, up_t[...].reshape(feat, width)) * (scale * scale * scale)
        h2[some] = h2_f.reshape(micro // 2, ROWS, width)
        return 0

    lax.fori_loop(0, 2, prepare, 0)

    def backward(m, _):
        @pl.when(s < last)
        def _():
            arrived(gb.at[m], bg, (m,))

        g = gb[m]
        g_f = g.astype(F32)
        w = (matmul(g, dn_n[...]) * q[m].astype(F32)).astype(BF16)
        mean = jnp.sum(g_f * kk[m], axis=1, keepdims=True)
        scale = sc[m][:, 0:1]
        mixed = matmul(w, up_t[...].reshape(feat, width))
        gi[m] = (g_f + scale * mixed - mean * h2[m]).astype(BF16)

        @pl.when(s > 0)
        def _():
            copy(gi.at[m], gb.at[m], bg, (m,), (s - 1, r)).start()

        wh[0, m] = w
        x = xb[m].astype(F32)
        xs[0, m] = (scale * x).astype(BF16)
        xs[1, m] = (x * (-(scale * scale * scale) * mean)).astype(BF16)
        return 0

    lax.fori_loop(0, micro, backward, 0)

    parts = (part_up, part_dn)
    rz, ry, z2, y2 = (rz_up, rz_dn), (ry_up, ry_dn), (rz2_up, rz2_dn), (ry2_up, ry2_dn)
    outs = (gu_out, gd_out)

    def part_y(a, e, part=slice(0, NZ)):
        return parts[a].at[part, at_y(e), 0:SPLIT[a]]

    def part_z(a, d):
        return parts[a].at[d % NZ, :, SPLIT[a]:]

    def add_into(ref, other):
        ref[...] = (ref[...].astype(F32) + other[...].astype(F32)).astype(BF16)

    def line_send(a, side, d, cond):
        send(part_z(a, (d, -d)[side]), ry[a].at[side, d - 1], ry1, (a, side, d - 1), (above, below)[side], cond)

    def first_sends(a):
        for side in range(2):
            half = slice(2 * side, 2 * side + 2)
            send(part_y(a, 4, half), rz[a].at[side, 0, half], rz1, (a, side, 0), (right, left)[side])
            for d in (3, 2, 1):
                line_send(a, side, d, (z == 0, z == NZ - 1)[side])

    def ring_step(a, k):
        for side in range(2):
            e = (4 - k, k - 4)[side]
            half = slice(2 * side, 2 * side + 2) if k == 1 else slice(0, NZ)
            got = rz[a].at[side, k - 1, half]
            arrived(got, rz1, (a, side, k - 1))
            add_into(part_y(a, e, half), got)
            if k < 4:
                send(part_y(a, e), rz[a].at[side, k], rz1, (a, side, k), (right, left)[side])

    def line_step(a, d):
        for side in range(2):
            way = (z, NZ - 1 - z)[side]
            got = ry[a].at[side, d]

            @pl.when((way >= 1) & (way <= NZ - 1 - d))
            def _():
                arrived(got, ry1, (a, side, d))
                add_into(part_z(a, (d, -d)[side]), got)

            if d > 0:
                line_send(a, side, d, (way >= 1) & (way <= NZ - 1 - d))

    rows = micro * ROWS
    for i in range(NZ):
        cols = slice(group * i, group * (i + 1))
        part_dn[i] = matmul(
            act[:, :, cols].reshape(rows, group), gb[...].reshape(rows, width), TN
        ).astype(BF16).reshape(part_dn.shape[1:])
    first_sends(1)
    for i in range(NZ):
        cols = slice(group * i, group * (i + 1))
        part_up[i] = matmul(
            wh[:, :, :, cols].reshape(2 * rows, group), xs[...].reshape(2 * rows, width), TN
        ).astype(BF16).reshape(part_up.shape[1:])
    first_sends(0)
    ring_step(1, 1)

    gg_acc[...] = jnp.zeros_like(gg_acc)

    def gain_rows(m, _):
        term = wh[0, m].astype(F32) * (wh[1, m].astype(F32) * sc[m][:, 0:1])
        gg_acc[...] += jnp.sum(term.reshape(ROWS // 8, 8, feat), axis=0)
        return 0

    lax.fori_loop(0, micro, gain_rows, 0)
    total = jnp.sum(gg_acc[...], axis=0, keepdims=True) / gain_row[...]
    gg_tot[...] = jnp.zeros_like(gg_tot)
    for d in range(NZ):
        for c in range(group // 128):
            gg_tot[0, at_z(d), c:c + 1, :] = total[:, group * d + 128 * c:group * d + 128 * (c + 1)]
    for d in range(1, NY):
        send(gg_tot.at[0], gg_y.at[d], hys, (d,), dev(z, at_y(d)))

    ring_step(0, 1)
    line_step(1, 2)
    line_step(0, 2)
    total = gg_tot[0]
    for d in range(1, NY):
        arrived(gg_y.at[d], hys, (d,))
        total = total + gg_y[d]
    gg_tot[1] = total
    for d in range(1, NZ):
        send(gg_tot.at[1], gg_z.at[d], hzs, (d,), dev(at_z(d), y))
    for k in (2, 3):
        for a in (1, 0):
            ring_step(a, k)
        for a in (1, 0):
            line_step(a, 3 - k)

    for a in (1, 0):
        kz = SPLIT[a]
        for d in range(1, NY):
            send(parts[a].at[0, at_y(d), kz:], y2[a].at[d], ry2, (a, d), dev(z, at_y(d)))
    for a in (1, 0):
        kz = SPLIT[a]
        ring_step(a, 4)
        for d in range(1, NZ):
            send(parts[a].at[d, y, 0:kz], z2[a].at[d], rz2, (a, d), dev(at_z(d), y))
    for a in (1, 0):
        kz = SPLIT[a]
        total = parts[a][0, y, kz:].astype(F32)
        for d in range(1, NY):
            arrived(y2[a].at[d], ry2, (a, d))
            total = total + y2[a][d].astype(F32)
        own[a, kz:] = total
    for a in (1, 0):
        kz = SPLIT[a]
        total = parts[a][0, y, 0:kz].astype(F32)
        for d in range(1, NZ):
            arrived(z2[a].at[d], rz2, (a, d))
            total = total + z2[a][d].astype(F32)
        own[a, 0:kz] = total
        outs[a][0] = own[a].T
    total = gg_tot[1]
    for d in range(1, NZ):
        arrived(gg_z.at[d], hzs, (d,))
        total = total + gg_z[d]
    gg_out[...] = total

    for c, cond in pending:
        if cond is None:
            c.wait_send()
        else:
            pl.when(cond)(c.wait_send)

    def drain(m, _):
        @pl.when(s < last)
        def _():
            copy(codes_out.at[m], xb.at[m], fx, (m,), (s + 1, r)).wait_send()

        @pl.when(s > 0)
        def _():
            copy(gi.at[m], gb.at[m], bg, (m,), (s - 1, r)).wait_send()

        return 0

    lax.fori_loop(0, micro, drain, 0)


def on_device(codes_in, cotangent, up, down, gain):
    rows, width = codes_in.shape
    piece = up.shape[2]
    feat = piece * lax.axis_size("replica")
    micro = rows // ROWS
    lanes = feat // NZ // 128
    offset = lax.axis_index("replica") * piece
    gain_p = lax.dynamic_update_slice(
        jnp.zeros((feat,), F32), gain[0].astype(F32), (offset,)
    ).reshape(NZ, lanes, 128)
    gain_p = jnp.pad(gain_p, ((0, 0), (0, 8 - lanes), (0, 0)))
    grid = (NZ, NY, piece, width)
    small = (NZ, 8, 128)

    def vm(shape, dtype=BF16):
        return pltpu.VMEM(shape, dtype)

    def sem(*shape):
        return pltpu.SemaphoreType.DMA((2,) + shape)

    ku, kd = SPLIT
    scratch = [
        vm(grid), vm(grid), vm((width, feat)), vm((width, feat)), vm((1, feat), F32),
        vm((micro, ROWS, width)), vm((micro, ROWS, width)), vm((micro, ROWS, width)),
        vm((micro, ROWS, feat)), vm((2, micro, ROWS, feat)), vm((micro, ROWS, feat)),
        vm((2, micro, ROWS, width)), vm((micro, ROWS, 128), F32),
        vm((micro, ROWS, width), F32), vm((micro, ROWS, width), F32),
        vm(grid), vm(grid),
        vm((2, 4, NZ, ku, width)), vm((2, 4, NZ, kd, width)),
        vm((2, NZ, NY, piece - ku, width)), vm((2, NZ, NY, piece - kd, width)),
        vm((NZ, ku, width)), vm((NZ, kd, width)),
        vm((NY, piece - ku, width)), vm((NY, piece - kd, width)),
        vm(small, F32), vm((NY,) + small, F32), vm((NZ,) + small, F32),
        vm((8, feat), F32), vm((2,) + small, F32), vm((NY,) + small, F32), vm((NZ,) + small, F32),
        vm((2, piece, width), F32),
        sem(2, NZ), sem(2, NY), sem(2, 2, 2, 4), sem(2, 2, 3), sem(NY), sem(NZ),
        sem(micro), sem(micro),
        sem(2, 2, 4), sem(2, 2, NZ), sem(2, NZ), sem(2, NY), sem(NY), sem(NZ),
    ]
    codes, grad_up, grad_dn, grad_gain = pl.pallas_call(
        kernel,
        out_shape=(
            jax.ShapeDtypeStruct((micro, ROWS, width), BF16),
            jax.ShapeDtypeStruct((1, width, piece), F32),
            jax.ShapeDtypeStruct((1, width, piece), F32),
            jax.ShapeDtypeStruct(small, F32),
        ),
        in_specs=[pl.BlockSpec(memory_space=pltpu.VMEM)] * 5,
        out_specs=tuple([pl.BlockSpec(memory_space=pltpu.VMEM)] * 4),
        scratch_shapes=scratch,
        compiler_params=pltpu.CompilerParams(
            collective_id=0, has_side_effects=True, vmem_limit_bytes=56 << 20
        ),
    )(codes_in, cotangent, up, down, gain_p)
    grad_gain = lax.dynamic_slice(grad_gain[:, :lanes].reshape(-1), (offset,), (piece,))
    return (codes.reshape(1, rows, width), grad_up, grad_dn, grad_gain[None])


def solution(mesh):
    placed = (
        P("replica", None),
        P("replica", None),
        P("section", None, "replica"),
        P("section", None, "replica"),
        P("section", "replica"),
    )
    return jax.shard_map(
        on_device,
        mesh=mesh,
        in_specs=placed,
        out_specs=(
            P("section", "replica", None),
            P("section", None, "replica"),
            P("section", None, "replica"),
            P("section", "replica"),
        ),
        check_vma=False,
    )
```

```python
import functools

import jax
import jax.numpy as jnp
from jax import lax
from jax.experimental import pallas as pl
from jax.experimental.pallas import tpu as pltpu
from jax.sharding import PartitionSpec as P

MESH = pl.DeviceIdType.MESH
EPS = 1e-06
NY, NZ = 8, 4
ROWS = 64
SPLIT = (48, 64)
SHORT = ((4, 3), (3, 4))
C0 = 0.7978845608028654
C1 = 0.044715
NN = (((1,), (0,)), ((), ()))
TN = (((0,), (0,)), ((), ()))
F32 = jnp.float32
BF16 = jnp.bfloat16


def matmul(a, b, dims=NN):
    return lax.dot_general(a, b, dims, preferred_element_type=F32)


def kernel(
    codes, cot, up_in, dn_in, gain_in,
    codes_out, gu_out, gd_out, gg_out,
    up_t, dn_t, up_n, dn_n, gain_row,
    xb, gb, gi, act, wh, q, xs, sc, kk, h2,
    part_up, part_dn, rz_up, rz_dn, ry_up, ry_dn, rz2_up, rz2_dn, ry2_up, ry2_dn,
    gain_own, gain_tot, gain_y, gain_z, gg_acc, gg_tot, gg_y, gg_z,
    zp1, yp1, zp2, yp2, gys, gzs, fx, bg, rz1, ry1, rz2, ry2, hys, hzs,
):
    last = lax.axis_size("section") - 1
    s = lax.axis_index("section")
    r = lax.axis_index("replica")
    y = lax.rem(r, NY)
    z = r // NY
    micro = xb.shape[0]
    feat = gain_row.shape[1]
    width = xb.shape[2]

    def at_y(d):
        return lax.rem(y + d + NY, NY)

    def at_z(d):
        return lax.rem(z + d + NZ, NZ)

    def dev(z_, y_):
        return (s, z_ * NY + y_)

    pending = []

    def copy(src, dst, sems, index, to):
        return pltpu.make_async_remote_copy(
            src_ref=src, dst_ref=dst,
            send_sem=sems.at[(0,) + index], recv_sem=sems.at[(1,) + index],
            device_id=to, device_id_type=MESH,
        )

    def send(src, dst, sems, index, to, cond=None):
        c = copy(src, dst, sems, index, to)
        if cond is None:
            c.start()
        else:
            pl.when(cond)(c.start)
        pending.append((c, cond))

    def arrived(dst, sems, index, cond=None):
        c = copy(dst, dst, sems, index, (s, r))
        if cond is None:
            c.wait_recv()
        else:
            pl.when(cond)(c.wait_recv)

    barrier = pltpu.get_barrier_semaphore()
    for d in range(1, NY):
        pl.semaphore_signal(barrier, inc=1, device_id=dev(z, at_y(d)), device_id_type=MESH)
    for d in range(1, NZ):
        pl.semaphore_signal(barrier, inc=1, device_id=dev(at_z(d), y), device_id_type=MESH)

    @pl.when(s > 0)
    def _():
        pl.semaphore_signal(barrier, inc=1, device_id=(s - 1, r), device_id_type=MESH)

    @pl.when(s < last)
    def _():
        pl.semaphore_signal(barrier, inc=1, device_id=(s + 1, r), device_id_type=MESH)

    pl.semaphore_wait(
        barrier, NY - 1 + NZ - 1 + jnp.where(s > 0, 1, 0) + jnp.where(s < last, 1, 0)
    )

    full = (up_t, dn_t)
    for a in range(2):
        full[a][0, y] = (up_in, dn_in)[a][...]

    row, cut = (5 * r) // 8, lax.rem(5 * r, 8)
    gain_own[...] = jnp.zeros_like(gain_own)
    piece = up_in.shape[0]
    for i in range(8):
        head = min(piece, 128 - 16 * i)

        @pl.when(cut == i)
        def _():
            gain = gain_in[...].astype(F32)
            gain_own[pl.ds(row, 1), 16 * i:16 * i + head] = gain[:, :head]
            if head < piece:
                gain_own[pl.ds(row + 1, 1), 0:piece - head] = gain[:, head:]

    def block_y(a, e, part=slice(0, NZ)):
        return full[a].at[part, at_y(e), 0:SPLIT[a]]

    def block_z(a, d):
        return full[a].at[d % NZ, :, SPLIT[a]:]

    right, left = dev(z, at_y(1)), dev(z, at_y(-1))
    above, below = dev(jnp.minimum(z + 1, NZ - 1), y), dev(jnp.maximum(z - 1, 0), y)
    first = (slice(0, 1), slice(0, 1))
    rest = (slice(1, NZ), slice(1, NZ))

    def ring(a, stream, side, k):
        if k < 3:
            return (first, rest)[stream][side]
        return ((slice(0, 1), None), (slice(1, 2), slice(2, NZ)))[stream][side]

    def ring_send(a, stream, side, k):
        part = ring(a, stream, side, k)
        if part is not None:
            e = (-k, k)[side]
            send(block_y(a, e, part), block_y(a, e, part), zp2, (a, stream, side, k), (right, left)[side])

    def short_send(a, side, k):
        if k < SHORT[a][side]:
            ref = full[a].at[0, at_y((-k, k)[side]), SPLIT[a]:]
            send(ref, ref, yp1, (a, side, k), (right, left)[side])

    def short_wait(a, side, k):
        if k < SHORT[a][side]:
            ref = full[a].at[0, at_y((-k - 1, k + 1)[side]), SPLIT[a]:]
            arrived(ref, yp1, (a, side, k))

    def ring_wait(a, stream, side, k):
        part = ring(a, stream, side, k)
        if part is not None:
            arrived(block_y(a, (-k - 1, k + 1)[side], part), zp2, (a, stream, side, k))

    for a in range(2):
        for side in range(2):
            short_send(a, side, 0)
    for a in range(2):
        kz = SPLIT[a]
        for d in range(1, NZ):
            send(full[a].at[0, y, 0:kz], full[a].at[NZ - d, y, 0:kz], zp1, (a, d), dev(at_z(d), y))
        for side in range(2):
            ring_send(a, 0, side, 0)
    for d in range(1, NY):
        send(gain_own, gain_y.at[d], gys, (d,), dev(z, at_y(d)))

    @pl.when(s == 0)
    def _():
        xb[...] = codes[...].reshape(xb.shape)

    @pl.when(s == last)
    def _():
        gb[...] = cot[...].reshape(gb.shape)

    def short_step(k):
        for a in range(2):
            for side in range(2):
                short_wait(a, side, k - 1)
                short_send(a, side, k)

    short_step(1)
    short_step(2)
    for a in range(2):
        for d in range(1, NZ):
            arrived(full[a].at[NZ - d, y, 0:SPLIT[a]], zp1, (a, d))
        for side in range(2):
            ring_send(a, 1, side, 0)
    short_step(3)
    short_step(4)
    for a in range(2):
        send(block_z(a, 0), block_z(a, -1), yp2, (a, 0, 0), above, z < NZ - 1)
        send(block_z(a, 0), block_z(a, 1), yp2, (a, 1, 0), below, z > 0)
    total = gain_own[...]
    for d in range(1, NY):
        arrived(gain_y.at[d], gys, (d,))
        total = total + gain_y[d]
    gain_tot[...] = total
    for d in range(1, NZ):
        send(gain_tot, gain_z.at[d], gzs, (d,), dev(at_z(d), y))
    for k in range(1, 4):
        for stream in range(2):
            for a in range(2):
                for side in range(2):
                    ring_wait(a, stream, side, k - 1)
                    ring_send(a, stream, side, k)
        for a in range(2):
            arrived(block_z(a, -k), yp2, (a, 0, k - 1), z >= k)
            if k < 3:
                send(block_z(a, -k), block_z(a, -k - 1), yp2, (a, 0, k), above, (z >= k) & (z < NZ - 1))
            arrived(block_z(a, k), yp2, (a, 1, k - 1), z <= NZ - 1 - k)
            if k < 3:
                send(block_z(a, k), block_z(a, k + 1), yp2, (a, 1, k), below, (z <= NZ - 1 - k) & (z > 0))
    for stream in range(2):
        for a in range(2):
            for side in range(2):
                ring_wait(a, stream, side, 3)
    total = gain_tot[...]
    for d in range(1, NZ):
        arrived(gain_z.at[d], gzs, (d,))
        total = total + gain_z[d]
    gain_z[0] = total
    group = feat // NZ
    for d in range(NZ):
        for c in range(group // 128):
            lane = group * d + 128 * c
            gain_row[:, lane:lane + 128] = gain_z[0, pl.ds(at_z(d) * (group // 128) + c, 1), :]

    for i in range(NZ):
        up_n[:, group * i:group * (i + 1)] = up_t[i].reshape(group, width).T

    def forward(m, _):
        @pl.when(s > 0)
        def _():
            arrived(xb.at[m], fx, (m,))

        x = xb[m]
        hidden = matmul(x, up_n[...])
        scale = lax.rsqrt(jnp.sum(hidden * hidden, axis=1, keepdims=True) * (1.0 / feat) + EPS)
        v = hidden * scale * gain_row[...]
        t = jnp.tanh(C0 * (v + C1 * (v * v * v)))
        a = (0.5 * v * (1.0 + t)).astype(BF16)
        out = (x.astype(F32) + matmul(a, dn_t[...].reshape(feat, width))).astype(BF16)
        codes_out[m] = out
        copy(codes_out.at[m], xb.at[m], fx, (m,), (s + 1, r)).start()
        slope = 0.5 * (1.0 + t) + (0.5 * C0) * v * (1.0 - t * t) * (1.0 + (3.0 * C1) * (v * v))
        q[m] = (slope * gain_row[...]).astype(BF16)
        act[m] = a
        wh[1, m] = hidden.astype(BF16)
        sc[m] = jnp.broadcast_to(scale, sc.shape[1:])
        return 0

    @pl.when(s < last)
    def _():
        lax.fori_loop(0, micro, forward, 0)


    def transpose_dn():
        for i in range(NZ):
            dn_n[:, group * i:group * (i + 1)] = dn_t[i].reshape(group, width).T

    def prepare(i, _):
        some = pl.ds(i * (micro // 2), micro // 2)
        rows = micro // 2 * ROWS
        h_b = wh[1, some].reshape(rows, feat)
        product = q[some].reshape(rows, feat).astype(F32) * h_b.astype(F32)
        scale = sc[some].reshape(rows, 128)[:, 0:1]
        kk_f = matmul(product.astype(BF16), dn_t[...].reshape(feat, width)) * (1.0 / feat)
        kk[some] = kk_f.reshape(micro // 2, ROWS, width)
        h2_f = matmul(h_b, up_t[...].reshape(feat, width)) * (scale * scale * scale)
        h2[some] = h2_f.reshape(micro // 2, ROWS, width)
        return 0

    @pl.when(s < last)
    def _():
        transpose_dn()
        lax.fori_loop(0, 2, prepare, 0)


    gg_acc[...] = jnp.zeros_like(gg_acc)

    def add_gain(m):
        term = wh[0, m].astype(F32) * (wh[1, m].astype(F32) * sc[m][:, 0:1])
        gg_acc[...] += jnp.sum(term.reshape(ROWS // 8, 8, feat), axis=0)

    def backward(m, _):
        arrived(gb.at[m], bg, (m,))
        g = gb[m]
        g_f = g.astype(F32)
        w = (matmul(g, dn_n[...]) * q[m].astype(F32)).astype(BF16)
        mean = jnp.sum(g_f * kk[m], axis=1, keepdims=True)
        scale = sc[m][:, 0:1]
        mixed = matmul(w, up_t[...].reshape(feat, width))
        gi[m] = (g_f + scale * mixed - mean * h2[m]).astype(BF16)

        @pl.when(s > 0)
        def _():
            copy(gi.at[m], gb.at[m], bg, (m,), (s - 1, r)).start()

        wh[0, m] = w
        x = xb[m].astype(F32)
        xs[0, m] = (scale * x).astype(BF16)
        xs[1, m] = (x * (-(scale * scale * scale) * mean)).astype(BF16)
        add_gain(m)
        return 0

    @pl.when(s < last)
    def _():
        lax.fori_loop(0, micro, backward, 0)

    def both(m, _):
        arrived(xb.at[m], fx, (m,))
        x = xb[m]
        hidden = matmul(x, up_n[...])
        scale = lax.rsqrt(jnp.sum(hidden * hidden, axis=1, keepdims=True) * (1.0 / feat) + EPS)
        v = hidden * scale * gain_row[...]
        t = jnp.tanh(C0 * (v + C1 * (v * v * v)))
        act[m] = (0.5 * v * (1.0 + t)).astype(BF16)
        slope = 0.5 * (1.0 + t) + (0.5 * C0) * v * (1.0 - t * t) * (1.0 + (3.0 * C1) * (v * v))
        w = wh[0, m].astype(F32) * (slope * gain_row[...])
        mean = jnp.sum(w * hidden, axis=1, keepdims=True) * (1.0 / feat)
        d_hid = (scale * (w - hidden * (scale * scale * mean))).astype(BF16)
        mixed = matmul(d_hid, up_t[...].reshape(feat, width))
        gi[m] = (gb[m].astype(F32) + mixed).astype(BF16)
        copy(gi.at[m], gb.at[m], bg, (m,), (s - 1, r)).start()
        wh[0, m] = w.astype(BF16)
        wh[1, m] = hidden.astype(BF16)
        sc[m] = jnp.broadcast_to(scale, sc.shape[1:])
        x = x.astype(F32)
        xs[0, m] = (scale * x).astype(BF16)
        xs[1, m] = (x * (-(scale * scale * scale) * mean)).astype(BF16)
        return 0

    @pl.when(s == last)
    def _():
        transpose_dn()
        half = micro // 2

        def ahead(i, _):
            some = pl.ds(i * half, half)
            d_act = matmul(gb[some].reshape(half * ROWS, width), dn_n[...])
            wh[0, some] = d_act.astype(BF16).reshape(half, ROWS, feat)
            return 0

        def after(i, _):
            some = pl.ds(i * half, half)
            a = act[some].reshape(half * ROWS, feat)
            mixed = matmul(a, dn_t[...].reshape(feat, width)).reshape(half, ROWS, width)
            codes_out[some] = (xb[some].astype(F32) + mixed).astype(BF16)
            for j in range(half):
                add_gain(i * half + j)
            return 0

        lax.fori_loop(0, 2, ahead, 0)
        lax.fori_loop(0, micro, both, 0)
        lax.fori_loop(0, 2, after, 0)


    parts = (part_up, part_dn)
    rz, ry, z2, y2 = (rz_up, rz_dn), (ry_up, ry_dn), (rz2_up, rz2_dn), (ry2_up, ry2_dn)
    outs = (gu_out, gd_out)

    def part_y(a, e, part=slice(0, NZ)):
        return parts[a].at[part, at_y(e), 0:SPLIT[a]]

    def part_z(a, d):
        return parts[a].at[d % NZ, :, SPLIT[a]:]

    def add_into(ref, other):
        ref[...] = (ref[...].astype(F32) + other[...].astype(F32)).astype(BF16)

    def line_send(a, side, d, cond):
        send(part_z(a, (d, -d)[side]), ry[a].at[side, d - 1], ry1, (a, side, d - 1), (above, below)[side], cond)

    def first_sends(a):
        for side in range(2):
            half = slice(2 * side, 2 * side + 2)
            send(part_y(a, 4, half), rz[a].at[side, 0, half], rz1, (a, side, 0), (right, left)[side])
            line_send(a, side, NZ - 1, (z == 0, z == NZ - 1)[side])

    def ring_step(a, k):
        for side in range(2):
            e = (4 - k, k - 4)[side]
            half = slice(2 * side, 2 * side + 2) if k == 1 else slice(0, NZ)
            got = rz[a].at[side, k - 1, half]
            arrived(got, rz1, (a, side, k - 1))
            add_into(part_y(a, e, half), got)
            if k < 4:
                send(part_y(a, e), rz[a].at[side, k], rz1, (a, side, k), (right, left)[side])

    def line_step(a, d):
        for side in range(2):
            way = (z, NZ - 1 - z)[side]
            got = ry[a].at[side, d]

            @pl.when((way >= 1) & (way <= NZ - 1 - d))
            def _():
                arrived(got, ry1, (a, side, d))
                add_into(part_z(a, (d, -d)[side]), got)

            if d > 0:
                line_send(a, side, d, way <= NZ - 1 - d)

    rows = micro * ROWS
    for i in range(NZ):
        cols = slice(group * i, group * (i + 1))
        part_dn[i] = matmul(
            act[:, :, cols].reshape(rows, group), gb[...].reshape(rows, width), TN
        ).astype(BF16).reshape(part_dn.shape[1:])
    first_sends(1)
    for i in range(NZ):
        cols = slice(group * i, group * (i + 1))
        part_up[i] = matmul(
            wh[:, :, :, cols].reshape(2 * rows, group), xs[...].reshape(2 * rows, width), TN
        ).astype(BF16).reshape(part_up.shape[1:])
    first_sends(0)
    ring_step(1, 1)

    total = jnp.sum(gg_acc[...], axis=0, keepdims=True) / gain_row[...]
    gg_tot[...] = jnp.zeros_like(gg_tot)
    for d in range(NZ):
        for c in range(group // 128):
            lane = group * d + 128 * c
            gg_tot[0, pl.ds(at_z(d) * (group // 128) + c, 1), :] = total[:, lane:lane + 128]
    for d in range(1, NY):
        send(gg_tot.at[0], gg_y.at[d], hys, (d,), dev(z, at_y(d)))

    ring_step(0, 1)
    line_step(1, 2)
    line_step(0, 2)
    total = gg_tot[0]
    for d in range(1, NY):
        arrived(gg_y.at[d], hys, (d,))
        total = total + gg_y[d]
    gg_tot[1] = total
    for d in range(1, NZ):
        send(gg_tot.at[1], gg_z.at[d], hzs, (d,), dev(at_z(d), y))
    for k in (2, 3):
        for a in (1, 0):
            ring_step(a, k)
        for a in (1, 0):
            line_step(a, 3 - k)

    for a in (1, 0):
        for d in range(1, NY):
            send(parts[a].at[0, at_y(d), SPLIT[a]:], y2[a].at[d], ry2, (a, d), dev(z, at_y(d)))
    for a in (1, 0):
        kz = SPLIT[a]
        ring_step(a, 4)
        for d in range(1, NZ):
            send(parts[a].at[d, y, 0:kz], z2[a].at[d], rz2, (a, d), dev(at_z(d), y))
    for a in (1, 0):
        kz = SPLIT[a]
        total = parts[a][0, y, kz:].astype(F32)
        for d in range(1, NY):
            arrived(y2[a].at[d], ry2, (a, d))
            total = total + y2[a][d].astype(F32)
        outs[a][kz:] = total
    for a in (1, 0):
        kz = SPLIT[a]
        total = parts[a][0, y, 0:kz].astype(F32)
        for d in range(1, NZ):
            arrived(z2[a].at[d], rz2, (a, d))
            total = total + z2[a][d].astype(F32)
        outs[a][0:kz] = total
    total = gg_tot[1]
    for d in range(1, NZ):
        arrived(gg_z.at[d], hzs, (d,))
        total = total + gg_z[d]
    gg_z[0] = total
    for i in range(8):
        head = min(piece, 128 - 16 * i)

        @pl.when(cut == i)
        def _():
            gg_out[:, 0:head] = gg_z[0, pl.ds(row, 1), 16 * i:16 * i + head]
            if head < piece:
                gg_out[:, head:] = gg_z[0, pl.ds(row + 1, 1), 0:piece - head]


    for c, cond in pending:
        if cond is None:
            c.wait_send()
        else:
            pl.when(cond)(c.wait_send)

    def drain(m, _):
        @pl.when(s < last)
        def _():
            copy(codes_out.at[m], xb.at[m], fx, (m,), (s + 1, r)).wait_send()

        @pl.when(s > 0)
        def _():
            copy(gi.at[m], gb.at[m], bg, (m,), (s - 1, r)).wait_send()

        return 0

    lax.fori_loop(0, micro, drain, 0)


def on_device(codes_in, cotangent, up, down, gain):
    rows, width = codes_in.shape
    piece = up.shape[2]
    feat = piece * lax.axis_size("replica")
    micro = rows // ROWS
    grid = (NZ, NY, piece, width)
    small = (-(-feat // 1024) * 8, 128)

    def vm(shape, dtype=BF16):
        return pltpu.VMEM(shape, dtype)

    def sem(*shape):
        return pltpu.SemaphoreType.DMA((2,) + shape)

    ku, kd = SPLIT
    scratch = [
        vm(grid), vm(grid), vm((width, feat)), vm((width, feat)), vm((1, feat), F32),
        vm((micro, ROWS, width)), vm((micro, ROWS, width)), vm((micro, ROWS, width)),
        vm((micro, ROWS, feat)), vm((2, micro, ROWS, feat)), vm((micro, ROWS, feat)),
        vm((2, micro, ROWS, width)), vm((micro, ROWS, 128), F32),
        vm((micro, ROWS, width), F32), vm((micro, ROWS, width), F32),
        vm(grid), vm(grid),
        vm((2, 4, NZ, ku, width)), vm((2, 4, NZ, kd, width)),
        vm((2, NZ, NY, piece - ku, width)), vm((2, NZ, NY, piece - kd, width)),
        vm((NZ, ku, width)), vm((NZ, kd, width)),
        vm((NY, piece - ku, width)), vm((NY, piece - kd, width)),
        vm(small, F32), vm(small, F32), vm((NY,) + small, F32), vm((NZ,) + small, F32),
        vm((8, feat), F32), vm((2,) + small, F32), vm((NY,) + small, F32), vm((NZ,) + small, F32),
        sem(2, NZ), sem(2, 2, 4), sem(2, 2, 2, 4), sem(2, 2, 3), sem(NY), sem(NZ),
        sem(micro), sem(micro),
        sem(2, 2, 4), sem(2, 2, NZ), sem(2, NZ), sem(2, NY), sem(NY), sem(NZ),
    ]
    codes, grad_up, grad_dn, grad_gain = pl.pallas_call(
        kernel,
        out_shape=(
            jax.ShapeDtypeStruct((micro, ROWS, width), BF16),
            jax.ShapeDtypeStruct((piece, width), F32),
            jax.ShapeDtypeStruct((piece, width), F32),
            jax.ShapeDtypeStruct((1, piece), F32),
        ),
        in_specs=[pl.BlockSpec(memory_space=pltpu.VMEM)] * 5,
        out_specs=tuple([pl.BlockSpec(memory_space=pltpu.VMEM)] * 4),
        scratch_shapes=scratch,
        compiler_params=pltpu.CompilerParams(
            collective_id=0, has_side_effects=True, vmem_limit_bytes=56 << 20
        ),
    )(codes_in, cotangent, up[0].T, down[0].T, gain)
    return (codes.reshape(1, rows, width), grad_up.T[None], grad_dn.T[None], grad_gain)


def solution(mesh):
    placed = (
        P("replica", None),
        P("replica", None),
        P("section", None, "replica"),
        P("section", None, "replica"),
        P("section", "replica"),
    )
    return jax.shard_map(
        on_device,
        mesh=mesh,
        in_specs=placed,
        out_specs=(
            P("section", "replica", None),
            P("section", None, "replica"),
            P("section", None, "replica"),
            P("section", "replica"),
        ),
        check_vma=False,
    )
```

```python
import functools

import jax
import jax.numpy as jnp
from jax import lax
from jax.experimental import pallas as pl
from jax.experimental.pallas import tpu as pltpu
from jax.sharding import PartitionSpec as P

MESH = pl.DeviceIdType.MESH
EPS = 1e-06
NY, NZ = 8, 4
ROWS = 64
SPLIT = (48, 64)
CUT = (48, 48)
SHORT = ((4, 3), (3, 4))
C0 = 0.7978845608028654
C1 = 0.044715
NN = (((1,), (0,)), ((), ()))
TN = (((0,), (0,)), ((), ()))
F32 = jnp.float32
BF16 = jnp.bfloat16


def matmul(a, b, dims=NN):
    return lax.dot_general(a, b, dims, preferred_element_type=F32)


def kernel(
    codes, cot, up_in, dn_in, gain_in,
    codes_out, gu_out, gd_out, gg_out,
    up_t, dn_t, up_n, dn_n, gain_row,
    xb, gb, gi, act, wh, q, xs, sc, kk, h2,
    part_up, part_dn, rz_up, rz_dn, ry_up, ry_dn, rz2_up, rz2_dn, ry2_up, ry2_dn,
    gain_own, gain_tot, gain_y, gain_z, gg_acc, gg_tot, gg_y, gg_z,
    zp1, yp1, zp2, yp2, gys, gzs, fx, bg, rz1, ry1, rz2, ry2, hys, hzs,
):
    last = lax.axis_size("section") - 1
    s = lax.axis_index("section")
    r = lax.axis_index("replica")
    y = lax.rem(r, NY)
    z = r // NY
    micro = xb.shape[0]
    feat = gain_row.shape[1]
    width = xb.shape[2]

    def at_y(d):
        return lax.rem(y + d + NY, NY)

    def at_z(d):
        return lax.rem(z + d + NZ, NZ)

    def dev(z_, y_):
        return (s, z_ * NY + y_)

    pending = []

    def copy(src, dst, sems, index, to):
        return pltpu.make_async_remote_copy(
            src_ref=src, dst_ref=dst,
            send_sem=sems.at[(0,) + index], recv_sem=sems.at[(1,) + index],
            device_id=to, device_id_type=MESH,
        )

    def send(src, dst, sems, index, to, cond=None):
        c = copy(src, dst, sems, index, to)
        if cond is None:
            c.start()
        else:
            pl.when(cond)(c.start)
        pending.append((c, cond))

    def arrived(dst, sems, index, cond=None):
        c = copy(dst, dst, sems, index, (s, r))
        if cond is None:
            c.wait_recv()
        else:
            pl.when(cond)(c.wait_recv)

    barrier = pltpu.get_barrier_semaphore()
    for d in range(1, NY):
        pl.semaphore_signal(barrier, inc=1, device_id=dev(z, at_y(d)), device_id_type=MESH)
    for d in range(1, NZ):
        pl.semaphore_signal(barrier, inc=1, device_id=dev(at_z(d), y), device_id_type=MESH)

    @pl.when(s > 0)
    def _():
        pl.semaphore_signal(barrier, inc=1, device_id=(s - 1, r), device_id_type=MESH)

    @pl.when(s < last)
    def _():
        pl.semaphore_signal(barrier, inc=1, device_id=(s + 1, r), device_id_type=MESH)

    pl.semaphore_wait(
        barrier, NY - 1 + NZ - 1 + jnp.where(s > 0, 1, 0) + jnp.where(s < last, 1, 0)
    )

    full = (up_t, dn_t)
    for a in range(2):
        full[a][0, y] = (up_in, dn_in)[a][...]

    row, cut = (5 * r) // 8, lax.rem(5 * r, 8)
    gain_own[...] = jnp.zeros_like(gain_own)
    piece = up_in.shape[0]
    for i in range(8):
        head = min(piece, 128 - 16 * i)

        @pl.when(cut == i)
        def _():
            gain = gain_in[...].astype(F32)
            gain_own[pl.ds(row, 1), 16 * i:16 * i + head] = gain[:, :head]
            if head < piece:
                gain_own[pl.ds(row + 1, 1), 0:piece - head] = gain[:, head:]

    def block_y(a, e, part=slice(0, NZ)):
        return full[a].at[part, at_y(e), 0:SPLIT[a]]

    def block_z(a, d):
        return full[a].at[d % NZ, :, SPLIT[a]:]

    right, left = dev(z, at_y(1)), dev(z, at_y(-1))
    above, below = dev(jnp.minimum(z + 1, NZ - 1), y), dev(jnp.maximum(z - 1, 0), y)
    first = (slice(0, 1), slice(0, 1))
    rest = (slice(1, NZ), slice(1, NZ))

    def ring(a, stream, side, k):
        if k < 3:
            return (first, rest)[stream][side]
        return ((slice(0, 1), None), (slice(1, 2), slice(2, NZ)))[stream][side]

    def ring_send(a, stream, side, k):
        part = ring(a, stream, side, k)
        if part is not None:
            e = (-k, k)[side]
            send(block_y(a, e, part), block_y(a, e, part), zp2, (a, stream, side, k), (right, left)[side])

    def short_send(a, side, k):
        if k < SHORT[a][side]:
            ref = full[a].at[0, at_y((-k, k)[side]), SPLIT[a]:]
            send(ref, ref, yp1, (a, side, k), (right, left)[side])

    def short_wait(a, side, k):
        if k < SHORT[a][side]:
            ref = full[a].at[0, at_y((-k - 1, k + 1)[side]), SPLIT[a]:]
            arrived(ref, yp1, (a, side, k))

    def ring_wait(a, stream, side, k):
        part = ring(a, stream, side, k)
        if part is not None:
            arrived(block_y(a, (-k - 1, k + 1)[side], part), zp2, (a, stream, side, k))

    for a in range(2):
        for side in range(2):
            short_send(a, side, 0)
    for a in range(2):
        kz = SPLIT[a]
        for d in range(1, NZ):
            send(full[a].at[0, y, 0:kz], full[a].at[NZ - d, y, 0:kz], zp1, (a, d), dev(at_z(d), y))
        for side in range(2):
            ring_send(a, 0, side, 0)
    for d in range(1, NY):
        send(gain_own, gain_y.at[d], gys, (d,), dev(z, at_y(d)))

    @pl.when(s == 0)
    def _():
        xb[...] = codes[...].reshape(xb.shape)

    @pl.when(s == last)
    def _():
        gb[...] = cot[...].reshape(gb.shape)

    def short_step(k):
        for a in range(2):
            for side in range(2):
                short_wait(a, side, k - 1)
                short_send(a, side, k)

    short_step(1)
    short_step(2)
    for a in range(2):
        for d in range(1, NZ):
            arrived(full[a].at[NZ - d, y, 0:SPLIT[a]], zp1, (a, d))
        for side in range(2):
            ring_send(a, 1, side, 0)
    short_step(3)
    short_step(4)
    for a in range(2):
        send(block_z(a, 0), block_z(a, -1), yp2, (a, 0, 0), above, z < NZ - 1)
        send(block_z(a, 0), block_z(a, 1), yp2, (a, 1, 0), below, z > 0)
    total = gain_own[...]
    for d in range(1, NY):
        arrived(gain_y.at[d], gys, (d,))
        total = total + gain_y[d]
    gain_tot[...] = total
    for d in range(1, NZ):
        send(gain_tot, gain_z.at[d], gzs, (d,), dev(at_z(d), y))
    for k in range(1, 4):
        for stream in range(2):
            for a in range(2):
                for side in range(2):
                    ring_wait(a, stream, side, k - 1)
                    ring_send(a, stream, side, k)
        for a in range(2):
            arrived(block_z(a, -k), yp2, (a, 0, k - 1), z >= k)
            if k < 3:
                send(block_z(a, -k), block_z(a, -k - 1), yp2, (a, 0, k), above, (z >= k) & (z < NZ - 1))
            arrived(block_z(a, k), yp2, (a, 1, k - 1), z <= NZ - 1 - k)
            if k < 3:
                send(block_z(a, k), block_z(a, k + 1), yp2, (a, 1, k), below, (z <= NZ - 1 - k) & (z > 0))
    for stream in range(2):
        for a in range(2):
            for side in range(2):
                ring_wait(a, stream, side, 3)
    total = gain_tot[...]
    for d in range(1, NZ):
        arrived(gain_z.at[d], gzs, (d,))
        total = total + gain_z[d]
    gain_z[0] = total
    group = feat // NZ
    for d in range(NZ):
        for c in range(group // 128):
            lane = group * d + 128 * c
            gain_row[:, lane:lane + 128] = gain_z[0, pl.ds(at_z(d) * (group // 128) + c, 1), :]

    for i in range(NZ):
        up_n[:, group * i:group * (i + 1)] = up_t[i].reshape(group, width).T

    def forward(m, _):
        @pl.when(s > 0)
        def _():
            arrived(xb.at[m], fx, (m,))

        x = xb[m]
        hidden = matmul(x, up_n[...])
        scale = lax.rsqrt(jnp.sum(hidden * hidden, axis=1, keepdims=True) * (1.0 / feat) + EPS)
        v = hidden * scale * gain_row[...]
        t = jnp.tanh(C0 * (v + C1 * (v * v * v)))
        a = (0.5 * v * (1.0 + t)).astype(BF16)
        out = (x.astype(F32) + matmul(a, dn_t[...].reshape(feat, width))).astype(BF16)
        codes_out[m] = out
        copy(codes_out.at[m], xb.at[m], fx, (m,), (s + 1, r)).start()
        slope = 0.5 * (1.0 + t) + (0.5 * C0) * v * (1.0 - t * t) * (1.0 + (3.0 * C1) * (v * v))
        q[m] = (slope * gain_row[...]).astype(BF16)
        act[m] = a
        wh[1, m] = hidden.astype(BF16)
        sc[m] = jnp.broadcast_to(scale, sc.shape[1:])
        return 0

    @pl.when(s < last)
    def _():
        lax.fori_loop(0, micro, forward, 0)


    def transpose_dn():
        for i in range(NZ):
            dn_n[:, group * i:group * (i + 1)] = dn_t[i].reshape(group, width).T

    def prepare(i, _):
        some = pl.ds(i * (micro // 2), micro // 2)
        rows = micro // 2 * ROWS
        h_b = wh[1, some].reshape(rows, feat)
        product = q[some].reshape(rows, feat).astype(F32) * h_b.astype(F32)
        scale = sc[some].reshape(rows, 128)[:, 0:1]
        kk_f = matmul(product.astype(BF16), dn_t[...].reshape(feat, width)) * (1.0 / feat)
        kk[some] = kk_f.reshape(micro // 2, ROWS, width)
        h2_f = matmul(h_b, up_t[...].reshape(feat, width)) * (scale * scale * scale)
        h2[some] = h2_f.reshape(micro // 2, ROWS, width)
        return 0

    @pl.when(s < last)
    def _():
        transpose_dn()
        lax.fori_loop(0, 2, prepare, 0)


    gg_acc[...] = jnp.zeros_like(gg_acc)

    def add_gain(m):
        term = wh[0, m].astype(F32) * (wh[1, m].astype(F32) * sc[m][:, 0:1])
        gg_acc[...] += jnp.sum(term.reshape(ROWS // 8, 8, feat), axis=0)

    half = micro // 2

    def backward(m, _, first):
        arrived(gb.at[m], bg, (m,))
        g = gb[m]
        g_f = g.astype(F32)
        w = (matmul(g, dn_n[...]) * q[m].astype(F32)).astype(BF16)
        mean = jnp.sum(g_f * kk[m], axis=1, keepdims=True)
        scale = sc[m][:, 0:1]
        if not first:
            mixed = matmul(w, up_t[...].reshape(feat, width))
            gi[m] = (g_f + scale * mixed - mean * h2[m]).astype(BF16)
            copy(gi.at[m], gb.at[m], bg, (m,), (s - 1, r)).start()
        wh[0, m] = w
        x = xb[m].astype(F32)
        xs[0, m] = (scale * x).astype(BF16)
        xs[1, m] = (x * (-(scale * scale * scale) * mean)).astype(BF16)

        if first:
            add_gain(m)
        return 0

    @pl.when(s == 0)
    def _():
        lax.fori_loop(0, micro, functools.partial(backward, first=True), 0)

    @pl.when((s > 0) & (s < last))
    def _():
        lax.fori_loop(0, micro, functools.partial(backward, first=False), 0)

    def both(m, _):
        arrived(xb.at[m], fx, (m,))
        x = xb[m]
        hidden = matmul(x, up_n[...])
        scale = lax.rsqrt(jnp.sum(hidden * hidden, axis=1, keepdims=True) * (1.0 / feat) + EPS)
        v = hidden * scale * gain_row[...]
        t = jnp.tanh(C0 * (v + C1 * (v * v * v)))
        act[m] = (0.5 * v * (1.0 + t)).astype(BF16)
        slope = 0.5 * (1.0 + t) + (0.5 * C0) * v * (1.0 - t * t) * (1.0 + (3.0 * C1) * (v * v))
        w = wh[0, m].astype(F32) * (slope * gain_row[...])
        mean = jnp.sum(w * hidden, axis=1, keepdims=True) * (1.0 / feat)
        d_hid = (scale * (w - hidden * (scale * scale * mean))).astype(BF16)
        mixed = matmul(d_hid, up_t[...].reshape(feat, width))
        gi[m] = (gb[m].astype(F32) + mixed).astype(BF16)
        copy(gi.at[m], gb.at[m], bg, (m,), (s - 1, r)).start()
        wh[0, m] = w.astype(BF16)
        wh[1, m] = hidden.astype(BF16)
        sc[m] = jnp.broadcast_to(scale, sc.shape[1:])
        x = x.astype(F32)
        xs[0, m] = (scale * x).astype(BF16)
        xs[1, m] = (x * (-(scale * scale * scale) * mean)).astype(BF16)
        return 0

    @pl.when(s == last)
    def _():
        transpose_dn()

        def ahead(i, _):
            some = pl.ds(i * half, half)
            d_act = matmul(gb[some].reshape(half * ROWS, width), dn_n[...])
            wh[0, some] = d_act.astype(BF16).reshape(half, ROWS, feat)
            return 0

        def after(i, _):
            some = pl.ds(i * half, half)
            a = act[some].reshape(half * ROWS, feat)
            mixed = matmul(a, dn_t[...].reshape(feat, width)).reshape(half, ROWS, width)
            codes_out[some] = (xb[some].astype(F32) + mixed).astype(BF16)
            return 0

        lax.fori_loop(0, 2, ahead, 0)
        lax.fori_loop(0, micro, both, 0)
        lax.fori_loop(0, 2, after, 0)

    parts = (part_up, part_dn)
    rz, ry, z2, y2 = (rz_up, rz_dn), (ry_up, ry_dn), (rz2_up, rz2_dn), (ry2_up, ry2_dn)
    outs = (gu_out, gd_out)

    def part_y(a, e, h):
        return parts[a].at[2 * h:2 * h + 2, at_y(e), 0:CUT[a]]

    def part_z(a, d, g):
        return parts[a].at[d % NZ, 4 * g:4 * g + 4, CUT[a]:]

    def add_into(ref, other):
        ref[...] = (ref[...].astype(F32) + other[...].astype(F32)).astype(BF16)

    def ring_step(a, k, halves=(0, 1)):
        for h in halves:
            for side in range(2):
                steps = 4 if h == side else 3
                if k > steps:
                    continue
                ref = part_y(a, (steps - k, k - steps)[side], h)
                if k > 0:
                    got = rz[a].at[side, h, k - 1]
                    arrived(got, rz1, (a, side, h, k - 1))
                    add_into(ref, got)
                if k < steps:
                    send(ref, rz[a].at[side, h, k], rz1, (a, side, h, k), (right, left)[side])

    def line_send(a, side, d, g, cond):
        dst = ry[a].at[side, d - 1, 4 * g:4 * g + 4]
        send(part_z(a, (d, -d)[side], g), dst, ry1, (a, side, d - 1, g), (above, below)[side], cond)

    def line_step(a, d):
        for g in range(2):
            for side in range(2):
                way = (z, NZ - 1 - z)[side]
                got = ry[a].at[side, d, 4 * g:4 * g + 4]

                @pl.when((way >= 1) & (way <= NZ - 1 - d))
                def _():
                    arrived(got, ry1, (a, side, d, g))
                    add_into(part_z(a, (d, -d)[side], g), got)

                if d > 0:
                    line_send(a, side, d, g, way <= NZ - 1 - d)

    tokens = micro * ROWS

    def fill(a, h):
        for i in (2 * h, 2 * h + 1):
            cols = slice(group * i, group * (i + 1))
            if a == 1:
                left = act[:, :, cols].reshape(tokens, group)
                right = gb[...].reshape(tokens, width)
            else:
                left = wh[:, :, :, cols].reshape(2 * tokens, group)
                right = xs[...].reshape(2 * tokens, width)
            parts[a][i] = matmul(left, right, TN).astype(BF16).reshape(part_up.shape[1:])
        ring_step(a, 0, (h,))

    for a in (1, 0):
        fill(a, 0)
        fill(a, 1)
        for side in range(2):
            for g in range(2):
                line_send(a, side, NZ - 1, g, (z == 0, z == NZ - 1)[side])
    ring_step(1, 1)

    @pl.when(s > 0)
    def _():
        def gain_of(m, _):
            add_gain(m)
            return 0

        lax.fori_loop(0, micro, gain_of, 0)

    total = jnp.sum(gg_acc[...], axis=0, keepdims=True) / gain_row[...]
    gg_tot[...] = jnp.zeros_like(gg_tot)
    for d in range(NZ):
        for c in range(group // 128):
            lane = group * d + 128 * c
            gg_tot[0, pl.ds(at_z(d) * (group // 128) + c, 1), :] = total[:, lane:lane + 128]
    for d in range(1, NY):
        send(gg_tot.at[0], gg_y.at[d], hys, (d,), dev(z, at_y(d)))

    ring_step(0, 1)
    line_step(1, 2)
    line_step(0, 2)
    total = gg_tot[0]
    for d in range(1, NY):
        arrived(gg_y.at[d], hys, (d,))
        total = total + gg_y[d]
    gg_tot[1] = total
    for d in range(1, NZ):
        send(gg_tot.at[1], gg_z.at[d], hzs, (d,), dev(at_z(d), y))
    for k in (2, 3):
        for a in (1, 0):
            ring_step(a, k)
        for a in (1, 0):
            line_step(a, 3 - k)

    for a in (1, 0):
        for d in range(1, NY):
            send(parts[a].at[0, at_y(d), CUT[a]:], y2[a].at[d], ry2, (a, d), dev(z, at_y(d)))
    for a in (1, 0):
        kz = CUT[a]
        ring_step(a, 4)
        for d in range(1, NZ):
            send(parts[a].at[d, y, 0:kz], z2[a].at[d], rz2, (a, d), dev(at_z(d), y))
    for a in (1, 0):
        kz = CUT[a]
        total = parts[a][0, y, kz:].astype(F32)
        for d in range(1, NY):
            arrived(y2[a].at[d], ry2, (a, d))
            total = total + y2[a][d].astype(F32)
        outs[a][kz:] = total
    for a in (1, 0):
        kz = CUT[a]
        total = parts[a][0, y, 0:kz].astype(F32)
        for d in range(1, NZ):
            arrived(z2[a].at[d], rz2, (a, d))
            total = total + z2[a][d].astype(F32)
        outs[a][0:kz] = total
    total = gg_tot[1]
    for d in range(1, NZ):
        arrived(gg_z.at[d], hzs, (d,))
        total = total + gg_z[d]
    gg_z[0] = total
    for i in range(8):
        head = min(piece, 128 - 16 * i)

        @pl.when(cut == i)
        def _():
            gg_out[:, 0:head] = gg_z[0, pl.ds(row, 1), 16 * i:16 * i + head]
            if head < piece:
                gg_out[:, head:] = gg_z[0, pl.ds(row + 1, 1), 0:piece - head]


    for c, cond in pending:
        if cond is None:
            c.wait_send()
        else:
            pl.when(cond)(c.wait_send)

    def drain(m, _):
        @pl.when(s < last)
        def _():
            copy(codes_out.at[m], xb.at[m], fx, (m,), (s + 1, r)).wait_send()

        @pl.when(s > 0)
        def _():
            copy(gi.at[m], gb.at[m], bg, (m,), (s - 1, r)).wait_send()

        return 0

    lax.fori_loop(0, micro, drain, 0)


def hand_over(*refs):
    count = len(refs) // 2
    sems = refs[-1]
    copies = [
        pltpu.make_async_copy(refs[i], refs[count + i], sems.at[i]) for i in range(count)
    ]
    for c in copies:
        c.start()
    for c in copies:
        c.wait()


def on_device(codes_in, cotangent, up, down, gain):
    rows, width = codes_in.shape
    piece = up.shape[2]
    feat = piece * lax.axis_size("replica")
    micro = rows // ROWS
    grid = (NZ, NY, piece, width)
    small = (-(-feat // 1024) * 8, 128)

    def vm(shape, dtype=BF16):
        return pltpu.VMEM(shape, dtype)

    def sem(*shape):
        return pltpu.SemaphoreType.DMA((2,) + shape)

    ku, kd = CUT
    scratch = [
        vm(grid), vm(grid), vm((width, feat)), vm((width, feat)), vm((1, feat), F32),
        vm((micro, ROWS, width)), vm((micro, ROWS, width)), vm((micro, ROWS, width)),
        vm((micro, ROWS, feat)), vm((2, micro, ROWS, feat)), vm((micro, ROWS, feat)),
        vm((2, micro, ROWS, width)), vm((micro, ROWS, 128), F32),
        vm((micro, ROWS, width), F32), vm((micro, ROWS, width), F32),
        vm(grid), vm(grid),
        vm((2, 2, 4, 2, ku, width)), vm((2, 2, 4, 2, kd, width)),
        vm((2, NZ, NY, piece - ku, width)), vm((2, NZ, NY, piece - kd, width)),
        vm((NZ, ku, width)), vm((NZ, kd, width)),
        vm((NY, piece - ku, width)), vm((NY, piece - kd, width)),
        vm(small, F32), vm(small, F32), vm((NY,) + small, F32), vm((NZ,) + small, F32),
        vm((8, feat), F32), vm((2,) + small, F32), vm((NY,) + small, F32), vm((NZ,) + small, F32),
        sem(2, NZ), sem(2, 2, 4), sem(2, 2, 2, 4), sem(2, 2, 3), sem(NY), sem(NZ),
        sem(micro), sem(micro),
        sem(2, 2, 2, 4), sem(2, 2, NZ, 2), sem(2, NZ), sem(2, NY), sem(NY), sem(NZ),
    ]
    results = pl.pallas_call(
        kernel,
        out_shape=(
            jax.ShapeDtypeStruct((micro, ROWS, width), BF16),
            jax.ShapeDtypeStruct((piece, width), F32),
            jax.ShapeDtypeStruct((piece, width), F32),
            jax.ShapeDtypeStruct((1, piece), F32),
        ),
        in_specs=[pl.BlockSpec(memory_space=pltpu.VMEM)] * 5,
        out_specs=tuple([pl.BlockSpec(memory_space=pltpu.VMEM)] * 4),
        scratch_shapes=scratch,
        compiler_params=pltpu.CompilerParams(
            collective_id=0, has_side_effects=True, vmem_limit_bytes=56 << 20
        ),
    )(codes_in, cotangent, up[0].T, down[0].T, gain)
    codes, grad_up, grad_dn, grad_gain = pl.pallas_call(
        hand_over,
        out_shape=tuple(jax.ShapeDtypeStruct(x.shape, x.dtype) for x in results),
        in_specs=[pl.BlockSpec(memory_space=pl.ANY)] * len(results),
        out_specs=tuple([pl.BlockSpec(memory_space=pl.ANY)] * len(results)),
        scratch_shapes=[pltpu.SemaphoreType.DMA((len(results),))],
    )(*results)
    return (codes.reshape(1, rows, width), grad_up.T[None], grad_dn.T[None], grad_gain)


def solution(mesh):
    placed = (
        P("replica", None),
        P("replica", None),
        P("section", None, "replica"),
        P("section", None, "replica"),
        P("section", "replica"),
    )
    return jax.shard_map(
        on_device,
        mesh=mesh,
        in_specs=placed,
        out_specs=(
            P("section", "replica", None),
            P("section", None, "replica"),
            P("section", None, "replica"),
            P("section", "replica"),
        ),
        check_vma=False,
    )
```

```python
import functools

import jax
import jax.numpy as jnp
from jax import lax
from jax.experimental import pallas as pl
from jax.experimental.pallas import tpu as pltpu
from jax.sharding import PartitionSpec as P

MESH = pl.DeviceIdType.MESH
EPS = 1e-06
NY, NZ = 8, 4
ROWS = 64
SPLIT = (48, 64)
CUT = (48, 48)
SHORT = ((4, 3), (3, 4))
C0 = 0.7978845608028654
C1 = 0.044715
NN = (((1,), (0,)), ((), ()))
TN = (((0,), (0,)), ((), ()))
F32 = jnp.float32
BF16 = jnp.bfloat16


def matmul(a, b, dims=NN):
    return lax.dot_general(a, b, dims, preferred_element_type=F32)


def kernel(
    codes, cot, up_in, dn_in, gain_in,
    codes_out, gu_out, gd_out, gg_out,
    up_t, dn_t, up_n, dn_n, gain_row,
    xb, gb, gi, act, wh, q, xs, sc, kk, h2,
    part_up, part_dn, rz_up, rz_dn, ry_up, ry_dn, rz2_up, rz2_dn, ry2_up, ry2_dn,
    gain_own, gain_tot, gain_y, gain_z, gg_acc, gg_tot, gg_y, gg_z,
    zp1, yp1, zp2, yp2, gys, gzs, fx, bg, rz1, ry1, rz2, ry2, hys, hzs, yb, io, wr,
):
    last = lax.axis_size("section") - 1
    s = lax.axis_index("section")
    r = lax.axis_index("replica")
    y = lax.rem(r, NY)
    z = r // NY
    micro = xb.shape[0]
    feat = gain_row.shape[1]
    width = xb.shape[2]

    def at_y(d):
        return lax.rem(y + d + NY, NY)

    def at_z(d):
        return lax.rem(z + d + NZ, NZ)

    def dev(z_, y_):
        return (s, z_ * NY + y_)

    pending = []

    def copy(src, dst, sems, index, to):
        return pltpu.make_async_remote_copy(
            src_ref=src, dst_ref=dst,
            send_sem=sems.at[(0,) + index], recv_sem=sems.at[(1,) + index],
            device_id=to, device_id_type=MESH,
        )

    def send(src, dst, sems, index, to, cond=None):
        c = copy(src, dst, sems, index, to)
        if cond is None:
            c.start()
        else:
            pl.when(cond)(c.start)
        pending.append((c, cond))

    def arrived(dst, sems, index, cond=None):
        c = copy(dst, dst, sems, index, (s, r))
        if cond is None:
            c.wait_recv()
        else:
            pl.when(cond)(c.wait_recv)

    fetch_codes = pltpu.make_async_copy(codes, xb, io.at[0])
    fetch_cot = pltpu.make_async_copy(cot, gb, io.at[1])
    pl.when(s == 0)(fetch_codes.start)
    pl.when(s == last)(fetch_cot.start)

    barrier = pltpu.get_barrier_semaphore()
    for d in range(1, NY):
        pl.semaphore_signal(barrier, inc=1, device_id=dev(z, at_y(d)), device_id_type=MESH)
    for d in range(1, NZ):
        pl.semaphore_signal(barrier, inc=1, device_id=dev(at_z(d), y), device_id_type=MESH)

    @pl.when(s > 0)
    def _():
        pl.semaphore_signal(barrier, inc=1, device_id=(s - 1, r), device_id_type=MESH)

    @pl.when(s < last)
    def _():
        pl.semaphore_signal(barrier, inc=1, device_id=(s + 1, r), device_id_type=MESH)

    pl.semaphore_wait(
        barrier, NY - 1 + NZ - 1 + jnp.where(s > 0, 1, 0) + jnp.where(s < last, 1, 0)
    )

    full = (up_t, dn_t)
    for a in range(2):
        full[a][0, y] = (up_in, dn_in)[a][...]

    row, cut = (5 * r) // 8, lax.rem(5 * r, 8)
    gain_own[...] = jnp.zeros_like(gain_own)
    piece = up_in.shape[0]
    for i in range(8):
        head = min(piece, 128 - 16 * i)

        @pl.when(cut == i)
        def _():
            gain = gain_in[...].astype(F32)
            gain_own[pl.ds(row, 1), 16 * i:16 * i + head] = gain[:, :head]
            if head < piece:
                gain_own[pl.ds(row + 1, 1), 0:piece - head] = gain[:, head:]

    def block_y(a, e, part=slice(0, NZ)):
        return full[a].at[part, at_y(e), 0:SPLIT[a]]

    def block_z(a, d):
        return full[a].at[d % NZ, :, SPLIT[a]:]

    right, left = dev(z, at_y(1)), dev(z, at_y(-1))
    above, below = dev(jnp.minimum(z + 1, NZ - 1), y), dev(jnp.maximum(z - 1, 0), y)
    first = (slice(0, 1), slice(0, 1))
    rest = (slice(1, NZ), slice(1, NZ))

    def ring(a, stream, side, k):
        if k < 3:
            return (first, rest)[stream][side]
        return ((slice(0, 1), None), (slice(1, 2), slice(2, NZ)))[stream][side]

    def ring_send(a, stream, side, k):
        part = ring(a, stream, side, k)
        if part is not None:
            e = (-k, k)[side]
            send(block_y(a, e, part), block_y(a, e, part), zp2, (a, stream, side, k), (right, left)[side])

    def short_send(a, side, k):
        if k < SHORT[a][side]:
            ref = full[a].at[0, at_y((-k, k)[side]), SPLIT[a]:]
            send(ref, ref, yp1, (a, side, k), (right, left)[side])

    def short_wait(a, side, k):
        if k < SHORT[a][side]:
            ref = full[a].at[0, at_y((-k - 1, k + 1)[side]), SPLIT[a]:]
            arrived(ref, yp1, (a, side, k))

    def ring_wait(a, stream, side, k):
        part = ring(a, stream, side, k)
        if part is not None:
            arrived(block_y(a, (-k - 1, k + 1)[side], part), zp2, (a, stream, side, k))

    for a in range(2):
        for side in range(2):
            short_send(a, side, 0)
    for a in range(2):
        kz = SPLIT[a]
        for d in range(1, NZ):
            send(full[a].at[0, y, 0:kz], full[a].at[NZ - d, y, 0:kz], zp1, (a, d), dev(at_z(d), y))
        for side in range(2):
            ring_send(a, 0, side, 0)
    for d in range(1, NY):
        send(gain_own, gain_y.at[d], gys, (d,), dev(z, at_y(d)))

    def short_step(k):
        for a in range(2):
            for side in range(2):
                short_wait(a, side, k - 1)
                short_send(a, side, k)

    short_step(1)
    short_step(2)
    for a in range(2):
        for d in range(1, NZ):
            arrived(full[a].at[NZ - d, y, 0:SPLIT[a]], zp1, (a, d))
        for side in range(2):
            ring_send(a, 1, side, 0)
    short_step(3)
    short_step(4)
    for a in range(2):
        send(block_z(a, 0), block_z(a, -1), yp2, (a, 0, 0), above, z < NZ - 1)
        send(block_z(a, 0), block_z(a, 1), yp2, (a, 1, 0), below, z > 0)
    total = gain_own[...]
    for d in range(1, NY):
        arrived(gain_y.at[d], gys, (d,))
        total = total + gain_y[d]
    gain_tot[...] = total
    for d in range(1, NZ):
        send(gain_tot, gain_z.at[d], gzs, (d,), dev(at_z(d), y))
    for k in range(1, 4):
        for stream in range(2):
            for a in range(2):
                for side in range(2):
                    ring_wait(a, stream, side, k - 1)
                    ring_send(a, stream, side, k)
        for a in range(2):
            arrived(block_z(a, -k), yp2, (a, 0, k - 1), z >= k)
            if k < 3:
                send(block_z(a, -k), block_z(a, -k - 1), yp2, (a, 0, k), above, (z >= k) & (z < NZ - 1))
            arrived(block_z(a, k), yp2, (a, 1, k - 1), z <= NZ - 1 - k)
            if k < 3:
                send(block_z(a, k), block_z(a, k + 1), yp2, (a, 1, k), below, (z <= NZ - 1 - k) & (z > 0))
    for stream in range(2):
        for a in range(2):
            for side in range(2):
                ring_wait(a, stream, side, 3)
    total = gain_tot[...]
    for d in range(1, NZ):
        arrived(gain_z.at[d], gzs, (d,))
        total = total + gain_z[d]
    gain_z[0] = total
    group = feat // NZ
    for d in range(NZ):
        for c in range(group // 128):
            lane = group * d + 128 * c
            gain_row[:, lane:lane + 128] = gain_z[0, pl.ds(at_z(d) * (group // 128) + c, 1), :]

    for i in range(NZ):
        up_n[:, group * i:group * (i + 1)] = up_t[i].reshape(group, width).T

    def forward(m, _):
        @pl.when(s > 0)
        def _():
            arrived(xb.at[m], fx, (m,))

        x = xb[m]
        hidden = matmul(x, up_n[...])
        scale = lax.rsqrt(jnp.sum(hidden * hidden, axis=1, keepdims=True) * (1.0 / feat) + EPS)
        v = hidden * scale * gain_row[...]
        t = jnp.tanh(C0 * (v + C1 * (v * v * v)))
        a = (0.5 * v * (1.0 + t)).astype(BF16)
        out = (x.astype(F32) + matmul(a, dn_t[...].reshape(feat, width))).astype(BF16)
        yb[m] = out
        copy(yb.at[m], xb.at[m], fx, (m,), (s + 1, r)).start()
        pltpu.make_async_copy(yb.at[m], codes_out.at[m], wr.at[m]).start()
        slope = 0.5 * (1.0 + t) + (0.5 * C0) * v * (1.0 - t * t) * (1.0 + (3.0 * C1) * (v * v))
        q[m] = (slope * gain_row[...]).astype(BF16)
        act[m] = a
        wh[1, m] = hidden.astype(BF16)
        sc[m] = jnp.broadcast_to(scale, sc.shape[1:])
        return 0

    pl.when(s == 0)(fetch_codes.wait)
    pl.when(s == last)(fetch_cot.wait)

    @pl.when(s < last)
    def _():
        lax.fori_loop(0, micro, forward, 0)


    def transpose_dn():
        for i in range(NZ):
            dn_n[:, group * i:group * (i + 1)] = dn_t[i].reshape(group, width).T

    def prepare(i, _):
        some = pl.ds(i * (micro // 2), micro // 2)
        rows = micro // 2 * ROWS
        h_b = wh[1, some].reshape(rows, feat)
        product = q[some].reshape(rows, feat).astype(F32) * h_b.astype(F32)
        scale = sc[some].reshape(rows, 128)[:, 0:1]
        kk_f = matmul(product.astype(BF16), dn_t[...].reshape(feat, width)) * (1.0 / feat)
        kk[some] = kk_f.reshape(micro // 2, ROWS, width)
        h2_f = matmul(h_b, up_t[...].reshape(feat, width)) * (scale * scale * scale)
        h2[some] = h2_f.reshape(micro // 2, ROWS, width)
        return 0

    @pl.when(s < last)
    def _():
        transpose_dn()
        lax.fori_loop(0, 2, prepare, 0)


    gg_acc[...] = jnp.zeros_like(gg_acc)

    def add_gain(m):
        term = wh[0, m].astype(F32) * (wh[1, m].astype(F32) * sc[m][:, 0:1])
        gg_acc[...] += jnp.sum(term.reshape(ROWS // 8, 8, feat), axis=0)

    half = micro // 2

    def backward(m, _, first):
        arrived(gb.at[m], bg, (m,))
        g = gb[m]
        g_f = g.astype(F32)
        w = (matmul(g, dn_n[...]) * q[m].astype(F32)).astype(BF16)
        mean = jnp.sum(g_f * kk[m], axis=1, keepdims=True)
        scale = sc[m][:, 0:1]
        if not first:
            mixed = matmul(w, up_t[...].reshape(feat, width))
            gi[m] = (g_f + scale * mixed - mean * h2[m]).astype(BF16)
            copy(gi.at[m], gb.at[m], bg, (m,), (s - 1, r)).start()
        wh[0, m] = w
        x = xb[m].astype(F32)
        xs[0, m] = (scale * x).astype(BF16)
        xs[1, m] = (x * (-(scale * scale * scale) * mean)).astype(BF16)

        if first:
            add_gain(m)
        return 0

    @pl.when(s == 0)
    def _():
        lax.fori_loop(0, micro, functools.partial(backward, first=True), 0)

    @pl.when((s > 0) & (s < last))
    def _():
        lax.fori_loop(0, micro, functools.partial(backward, first=False), 0)

    def both(m, _):
        arrived(xb.at[m], fx, (m,))
        x = xb[m]
        hidden = matmul(x, up_n[...])
        scale = lax.rsqrt(jnp.sum(hidden * hidden, axis=1, keepdims=True) * (1.0 / feat) + EPS)
        v = hidden * scale * gain_row[...]
        t = jnp.tanh(C0 * (v + C1 * (v * v * v)))
        act[m] = (0.5 * v * (1.0 + t)).astype(BF16)
        slope = 0.5 * (1.0 + t) + (0.5 * C0) * v * (1.0 - t * t) * (1.0 + (3.0 * C1) * (v * v))
        w = wh[0, m].astype(F32) * (slope * gain_row[...])
        mean = jnp.sum(w * hidden, axis=1, keepdims=True) * (1.0 / feat)
        d_hid = (scale * (w - hidden * (scale * scale * mean))).astype(BF16)
        mixed = matmul(d_hid, up_t[...].reshape(feat, width))
        gi[m] = (gb[m].astype(F32) + mixed).astype(BF16)
        copy(gi.at[m], gb.at[m], bg, (m,), (s - 1, r)).start()
        wh[0, m] = w.astype(BF16)
        wh[1, m] = hidden.astype(BF16)
        sc[m] = jnp.broadcast_to(scale, sc.shape[1:])
        x = x.astype(F32)
        xs[0, m] = (scale * x).astype(BF16)
        xs[1, m] = (x * (-(scale * scale * scale) * mean)).astype(BF16)
        return 0

    @pl.when(s == last)
    def _():
        transpose_dn()

        def ahead(i, _):
            some = pl.ds(i * half, half)
            d_act = matmul(gb[some].reshape(half * ROWS, width), dn_n[...])
            wh[0, some] = d_act.astype(BF16).reshape(half, ROWS, feat)
            return 0

        def after(i, _):
            some = pl.ds(i * half, half)
            a = act[some].reshape(half * ROWS, feat)
            mixed = matmul(a, dn_t[...].reshape(feat, width)).reshape(half, ROWS, width)
            yb[some] = (xb[some].astype(F32) + mixed).astype(BF16)
            for j in range(half):
                m = i * half + j
                pltpu.make_async_copy(yb.at[m], codes_out.at[m], wr.at[m]).start()
            return 0

        lax.fori_loop(0, 2, ahead, 0)
        lax.fori_loop(0, micro, both, 0)
        lax.fori_loop(0, 2, after, 0)

    parts = (part_up, part_dn)
    rz, ry, z2, y2 = (rz_up, rz_dn), (ry_up, ry_dn), (rz2_up, rz2_dn), (ry2_up, ry2_dn)
    outs = (gu_out, gd_out)

    def part_y(a, e, h):
        return parts[a].at[2 * h:2 * h + 2, at_y(e), 0:CUT[a]]

    def part_z(a, d, g):
        return parts[a].at[d % NZ, 4 * g:4 * g + 4, CUT[a]:]

    def add_into(ref, other):
        ref[...] = (ref[...].astype(F32) + other[...].astype(F32)).astype(BF16)

    def ring_step(a, k, halves=(0, 1)):
        for h in halves:
            for side in range(2):
                steps = 4 if h == side else 3
                if k > steps:
                    continue
                ref = part_y(a, (steps - k, k - steps)[side], h)
                if k > 0:
                    got = rz[a].at[side, h, k - 1]
                    arrived(got, rz1, (a, side, h, k - 1))
                    add_into(ref, got)
                if k < steps:
                    send(ref, rz[a].at[side, h, k], rz1, (a, side, h, k), (right, left)[side])

    def line_send(a, side, d, g, cond):
        dst = ry[a].at[side, d - 1, 4 * g:4 * g + 4]
        send(part_z(a, (d, -d)[side], g), dst, ry1, (a, side, d - 1, g), (above, below)[side], cond)

    def line_step(a, d):
        for g in range(2):
            for side in range(2):
                way = (z, NZ - 1 - z)[side]
                got = ry[a].at[side, d, 4 * g:4 * g + 4]

                @pl.when((way >= 1) & (way <= NZ - 1 - d))
                def _():
                    arrived(got, ry1, (a, side, d, g))
                    add_into(part_z(a, (d, -d)[side], g), got)

                if d > 0:
                    line_send(a, side, d, g, way <= NZ - 1 - d)

    tokens = micro * ROWS

    def fill(a, h):
        for i in (2 * h, 2 * h + 1):
            cols = slice(group * i, group * (i + 1))
            if a == 1:
                left = act[:, :, cols].reshape(tokens, group)
                right = gb[...].reshape(tokens, width)
            else:
                left = wh[:, :, :, cols].reshape(2 * tokens, group)
                right = xs[...].reshape(2 * tokens, width)
            parts[a][i] = matmul(left, right, TN).astype(BF16).reshape(part_up.shape[1:])
        ring_step(a, 0, (h,))

    for a in (1, 0):
        fill(a, 0)
        fill(a, 1)
        for side in range(2):
            for g in range(2):
                line_send(a, side, NZ - 1, g, (z == 0, z == NZ - 1)[side])
    ring_step(1, 1)

    @pl.when(s > 0)
    def _():
        def gain_of(m, _):
            add_gain(m)
            return 0

        lax.fori_loop(0, micro, gain_of, 0)

    total = jnp.sum(gg_acc[...], axis=0, keepdims=True) / gain_row[...]
    gg_tot[...] = jnp.zeros_like(gg_tot)
    for d in range(NZ):
        for c in range(group // 128):
            lane = group * d + 128 * c
            gg_tot[0, pl.ds(at_z(d) * (group // 128) + c, 1), :] = total[:, lane:lane + 128]
    for d in range(1, NY):
        send(gg_tot.at[0], gg_y.at[d], hys, (d,), dev(z, at_y(d)))

    ring_step(0, 1)
    line_step(1, 2)
    line_step(0, 2)
    total = gg_tot[0]
    for d in range(1, NY):
        arrived(gg_y.at[d], hys, (d,))
        total = total + gg_y[d]
    gg_tot[1] = total
    for d in range(1, NZ):
        send(gg_tot.at[1], gg_z.at[d], hzs, (d,), dev(at_z(d), y))
    for k in (2, 3):
        for a in (1, 0):
            ring_step(a, k)
        for a in (1, 0):
            line_step(a, 3 - k)

    for a in (1, 0):
        for d in range(1, NY):
            send(parts[a].at[0, at_y(d), CUT[a]:], y2[a].at[d], ry2, (a, d), dev(z, at_y(d)))
    for a in (1, 0):
        kz = CUT[a]
        ring_step(a, 4)
        for d in range(1, NZ):
            send(parts[a].at[d, y, 0:kz], z2[a].at[d], rz2, (a, d), dev(at_z(d), y))
    for a in (1, 0):
        kz = CUT[a]
        total = parts[a][0, y, kz:].astype(F32)
        for d in range(1, NY):
            arrived(y2[a].at[d], ry2, (a, d))
            total = total + y2[a][d].astype(F32)
        outs[a][kz:] = total
    for a in (1, 0):
        kz = CUT[a]
        total = parts[a][0, y, 0:kz].astype(F32)
        for d in range(1, NZ):
            arrived(z2[a].at[d], rz2, (a, d))
            total = total + z2[a][d].astype(F32)
        outs[a][0:kz] = total
    total = gg_tot[1]
    for d in range(1, NZ):
        arrived(gg_z.at[d], hzs, (d,))
        total = total + gg_z[d]
    gg_z[0] = total
    for i in range(8):
        head = min(piece, 128 - 16 * i)

        @pl.when(cut == i)
        def _():
            gg_out[:, 0:head] = gg_z[0, pl.ds(row, 1), 16 * i:16 * i + head]
            if head < piece:
                gg_out[:, head:] = gg_z[0, pl.ds(row + 1, 1), 0:piece - head]


    for c, cond in pending:
        if cond is None:
            c.wait_send()
        else:
            pl.when(cond)(c.wait_send)

    def drain(m, _):
        pltpu.make_async_copy(yb.at[m], codes_out.at[m], wr.at[m]).wait()

        @pl.when(s < last)
        def _():
            copy(yb.at[m], xb.at[m], fx, (m,), (s + 1, r)).wait_send()

        @pl.when(s > 0)
        def _():
            copy(gi.at[m], gb.at[m], bg, (m,), (s - 1, r)).wait_send()

        return 0

    lax.fori_loop(0, micro, drain, 0)


def hand_over(*refs):
    count = len(refs) // 2
    for i in range(count):
        refs[count + i][...] = refs[i][...]


def on_device(codes_in, cotangent, up, down, gain):
    rows, width = codes_in.shape
    piece = up.shape[2]
    feat = piece * lax.axis_size("replica")
    micro = rows // ROWS
    grid = (NZ, NY, piece, width)
    small = (-(-feat // 1024) * 8, 128)

    def vm(shape, dtype=BF16):
        return pltpu.VMEM(shape, dtype)

    def sem(*shape):
        return pltpu.SemaphoreType.DMA((2,) + shape)

    ku, kd = CUT
    scratch = [
        vm(grid), vm(grid), vm((width, feat)), vm((width, feat)), vm((1, feat), F32),
        vm((micro, ROWS, width)), vm((micro, ROWS, width)), vm((micro, ROWS, width)),
        vm((micro, ROWS, feat)), vm((2, micro, ROWS, feat)), vm((micro, ROWS, feat)),
        vm((2, micro, ROWS, width)), vm((micro, ROWS, 128), F32),
        vm((micro, ROWS, width), F32), vm((micro, ROWS, width), F32),
        vm(grid), vm(grid),
        vm((2, 2, 4, 2, ku, width)), vm((2, 2, 4, 2, kd, width)),
        vm((2, NZ, NY, piece - ku, width)), vm((2, NZ, NY, piece - kd, width)),
        vm((NZ, ku, width)), vm((NZ, kd, width)),
        vm((NY, piece - ku, width)), vm((NY, piece - kd, width)),
        vm(small, F32), vm(small, F32), vm((NY,) + small, F32), vm((NZ,) + small, F32),
        vm((8, feat), F32), vm((2,) + small, F32), vm((NY,) + small, F32), vm((NZ,) + small, F32),
        sem(2, NZ), sem(2, 2, 4), sem(2, 2, 2, 4), sem(2, 2, 3), sem(NY), sem(NZ),
        sem(micro), sem(micro),
        sem(2, 2, 2, 4), sem(2, 2, NZ, 2), sem(2, NZ), sem(2, NY), sem(NY), sem(NZ),
        vm((micro, ROWS, width)), pltpu.SemaphoreType.DMA((2,)), pltpu.SemaphoreType.DMA((micro,)),
    ]
    results = pl.pallas_call(
        kernel,
        out_shape=(
            jax.ShapeDtypeStruct((micro, ROWS, width), BF16),
            jax.ShapeDtypeStruct((piece, width), F32),
            jax.ShapeDtypeStruct((piece, width), F32),
            jax.ShapeDtypeStruct((1, piece), F32),
        ),
        in_specs=[pl.BlockSpec(memory_space=pl.ANY)] * 2 + [pl.BlockSpec(memory_space=pltpu.VMEM)] * 3,
        out_specs=(pl.BlockSpec(memory_space=pl.ANY),) + (pl.BlockSpec(memory_space=pltpu.VMEM),) * 3,
        scratch_shapes=scratch,
        compiler_params=pltpu.CompilerParams(
            collective_id=0, has_side_effects=True, vmem_limit_bytes=56 << 20
        ),
    )(codes_in.reshape(micro, ROWS, width), cotangent.reshape(micro, ROWS, width), up[0].T, down[0].T, gain)
    codes, grad_up, grad_dn, grad_gain = pl.pallas_call(
        hand_over,
        out_shape=tuple(jax.ShapeDtypeStruct(x.shape, x.dtype) for x in results),
        in_specs=[pl.BlockSpec(memory_space=pltpu.VMEM)] * len(results),
        out_specs=tuple([pl.BlockSpec(memory_space=pltpu.VMEM)] * len(results)),
    )(*results)
    return (codes.reshape(1, rows, width), grad_up.T[None], grad_dn.T[None], grad_gain)


def solution(mesh):
    placed = (
        P("replica", None),
        P("replica", None),
        P("section", None, "replica"),
        P("section", None, "replica"),
        P("section", "replica"),
    )
    return jax.shard_map(
        on_device,
        mesh=mesh,
        in_specs=placed,
        out_specs=(
            P("section", "replica", None),
            P("section", None, "replica"),
            P("section", None, "replica"),
            P("section", "replica"),
        ),
        check_vma=False,
    )
```

```python
import functools

import jax
import jax.numpy as jnp
from jax import lax
from jax.experimental import pallas as pl
from jax.experimental.pallas import tpu as pltpu
from jax.sharding import PartitionSpec as P

MESH = pl.DeviceIdType.MESH
EPS = 1e-06
NY, NZ = 8, 4
ROWS = 64
SPLIT = (48, 64)
CUT = (48, 48)
SHORT = ((4, 3), (3, 4))
C0 = 0.7978845608028654
C1 = 0.044715
NN = (((1,), (0,)), ((), ()))
TN = (((0,), (0,)), ((), ()))
F32 = jnp.float32
BF16 = jnp.bfloat16


def matmul(a, b, dims=NN):
    return lax.dot_general(a, b, dims, preferred_element_type=F32)


def kernel(
    codes, cot, up_in, dn_in, gain_in,
    codes_out, gu_out, gd_out, gg_out,
    up_t, dn_t, up_n, dn_n, gain_row,
    xb, gb, gi, act, wh, q, xs, sc, kk, h2,
    part_up, part_dn, rz_up, rz_dn, ry_up, ry_dn, rz2_up, rz2_dn, ry2_up, ry2_dn,
    gain_own, gain_tot, gain_y, gain_z, gg_acc, gg_tot, gg_y, gg_z,
    zp1, yp1, zp2, yp2, gys, gzs, fx, bg, rz1, ry1, rz2, ry2, hys, hzs, yb, io, wr,
):
    last = lax.axis_size("section") - 1
    s = lax.axis_index("section")
    r = lax.axis_index("replica")
    y = lax.rem(r, NY)
    z = r // NY
    micro = xb.shape[0]
    feat = gain_row.shape[1]
    width = xb.shape[2]

    def at_y(d):
        return lax.rem(y + d + NY, NY)

    def at_z(d):
        return lax.rem(z + d + NZ, NZ)

    def dev(z_, y_):
        return (s, z_ * NY + y_)

    pending = []

    def copy(src, dst, sems, index, to):
        return pltpu.make_async_remote_copy(
            src_ref=src, dst_ref=dst,
            send_sem=sems.at[(0,) + index], recv_sem=sems.at[(1,) + index],
            device_id=to, device_id_type=MESH,
        )

    def send(src, dst, sems, index, to, cond=None):
        c = copy(src, dst, sems, index, to)
        if cond is None:
            c.start()
        else:
            pl.when(cond)(c.start)
        pending.append((c, cond))

    def arrived(dst, sems, index, cond=None):
        c = copy(dst, dst, sems, index, (s, r))
        if cond is None:
            c.wait_recv()
        else:
            pl.when(cond)(c.wait_recv)

    fetch_codes = pltpu.make_async_copy(codes, xb, io.at[0])
    fetch_cot = pltpu.make_async_copy(cot, gb, io.at[1])
    pl.when(s == 0)(fetch_codes.start)
    pl.when(s == last)(fetch_cot.start)

    barrier = pltpu.get_barrier_semaphore()
    for d in range(1, NY):
        pl.semaphore_signal(barrier, inc=1, device_id=dev(z, at_y(d)), device_id_type=MESH)
    for d in range(1, NZ):
        pl.semaphore_signal(barrier, inc=1, device_id=dev(at_z(d), y), device_id_type=MESH)

    @pl.when(s > 0)
    def _():
        pl.semaphore_signal(barrier, inc=1, device_id=(s - 1, r), device_id_type=MESH)

    @pl.when(s < last)
    def _():
        pl.semaphore_signal(barrier, inc=1, device_id=(s + 1, r), device_id_type=MESH)

    full = (up_t, dn_t)
    for a in range(2):
        full[a][0, y] = (up_in, dn_in)[a][...]

    row, cut = (5 * r) // 8, lax.rem(5 * r, 8)
    gain_own[...] = jnp.zeros_like(gain_own)
    piece = up_in.shape[0]
    for i in range(8):
        head = min(piece, 128 - 16 * i)

        @pl.when(cut == i)
        def _():
            gain = gain_in[...].astype(F32)
            gain_own[pl.ds(row, 1), 16 * i:16 * i + head] = gain[:, :head]
            if head < piece:
                gain_own[pl.ds(row + 1, 1), 0:piece - head] = gain[:, head:]

    pl.semaphore_wait(
        barrier, NY - 1 + NZ - 1 + jnp.where(s > 0, 1, 0) + jnp.where(s < last, 1, 0)
    )

    def block_y(a, e, part=slice(0, NZ)):
        return full[a].at[part, at_y(e), 0:SPLIT[a]]

    def block_z(a, d):
        return full[a].at[d % NZ, :, SPLIT[a]:]

    right, left = dev(z, at_y(1)), dev(z, at_y(-1))
    above, below = dev(jnp.minimum(z + 1, NZ - 1), y), dev(jnp.maximum(z - 1, 0), y)
    first = (slice(0, 1), slice(0, 1))
    rest = (slice(1, NZ), slice(1, NZ))

    def ring(a, stream, side, k):
        if k < 3:
            return (first, rest)[stream][side]
        return ((slice(0, 1), None), (slice(1, 2), slice(2, NZ)))[stream][side]

    def ring_send(a, stream, side, k):
        part = ring(a, stream, side, k)
        if part is not None:
            e = (-k, k)[side]
            send(block_y(a, e, part), block_y(a, e, part), zp2, (a, stream, side, k), (right, left)[side])

    def short_send(a, side, k):
        if k < SHORT[a][side]:
            ref = full[a].at[0, at_y((-k, k)[side]), SPLIT[a]:]
            send(ref, ref, yp1, (a, side, k), (right, left)[side])

    def short_wait(a, side, k):
        if k < SHORT[a][side]:
            ref = full[a].at[0, at_y((-k - 1, k + 1)[side]), SPLIT[a]:]
            arrived(ref, yp1, (a, side, k))

    def ring_wait(a, stream, side, k):
        part = ring(a, stream, side, k)
        if part is not None:
            arrived(block_y(a, (-k - 1, k + 1)[side], part), zp2, (a, stream, side, k))

    for a in range(2):
        for side in range(2):
            short_send(a, side, 0)
    for a in range(2):
        kz = SPLIT[a]
        for d in range(1, NZ):
            send(full[a].at[0, y, 0:kz], full[a].at[NZ - d, y, 0:kz], zp1, (a, d), dev(at_z(d), y))
        for side in range(2):
            ring_send(a, 0, side, 0)
    for d in range(1, NY):
        send(gain_own, gain_y.at[d], gys, (d,), dev(z, at_y(d)))

    def short_step(k):
        for a in range(2):
            for side in range(2):
                short_wait(a, side, k - 1)
                short_send(a, side, k)

    short_step(1)
    short_step(2)
    for a in range(2):
        for d in range(1, NZ):
            arrived(full[a].at[NZ - d, y, 0:SPLIT[a]], zp1, (a, d))
        for side in range(2):
            ring_send(a, 1, side, 0)
    short_step(3)
    short_step(4)
    for a in range(2):
        send(block_z(a, 0), block_z(a, -1), yp2, (a, 0, 0), above, z < NZ - 1)
        send(block_z(a, 0), block_z(a, 1), yp2, (a, 1, 0), below, z > 0)
    total = gain_own[...]
    for d in range(1, NY):
        arrived(gain_y.at[d], gys, (d,))
        total = total + gain_y[d]
    gain_tot[...] = total
    for d in range(1, NZ):
        send(gain_tot, gain_z.at[d], gzs, (d,), dev(at_z(d), y))
    for k in range(1, 4):
        for stream in range(2):
            for a in range(2):
                for side in range(2):
                    ring_wait(a, stream, side, k - 1)
                    ring_send(a, stream, side, k)
        for a in range(2):
            arrived(block_z(a, -k), yp2, (a, 0, k - 1), z >= k)
            if k < 3:
                send(block_z(a, -k), block_z(a, -k - 1), yp2, (a, 0, k), above, (z >= k) & (z < NZ - 1))
            arrived(block_z(a, k), yp2, (a, 1, k - 1), z <= NZ - 1 - k)
            if k < 3:
                send(block_z(a, k), block_z(a, k + 1), yp2, (a, 1, k), below, (z <= NZ - 1 - k) & (z > 0))
    for stream in range(2):
        for side in range(2):
            ring_wait(0, stream, side, 3)
    total = gain_tot[...]
    for d in range(1, NZ):
        arrived(gain_z.at[d], gzs, (d,))
        total = total + gain_z[d]
    gain_z[0] = total
    group = feat // NZ
    for d in range(NZ):
        for c in range(group // 128):
            lane = group * d + 128 * c
            gain_row[:, lane:lane + 128] = gain_z[0, pl.ds(at_z(d) * (group // 128) + c, 1), :]

    for i in range(NZ):
        up_n[:, group * i:group * (i + 1)] = up_t[i].reshape(group, width).T
    for stream in range(2):
        for side in range(2):
            ring_wait(1, stream, side, 3)

    def transpose_dn():
        for i in range(NZ):
            dn_n[:, group * i:group * (i + 1)] = dn_t[i].reshape(group, width).T

    pl.when(s > 0)(transpose_dn)

    def forward(m, _):
        @pl.when(s > 0)
        def _():
            arrived(xb.at[m], fx, (m,))

        x = xb[m]
        hidden = matmul(x, up_n[...])
        scale = lax.rsqrt(jnp.sum(hidden * hidden, axis=1, keepdims=True) * (1.0 / feat) + EPS)
        v = hidden * scale * gain_row[...]
        t = jnp.tanh(C0 * (v + C1 * (v * v * v)))
        a = (0.5 * v * (1.0 + t)).astype(BF16)
        out = (x.astype(F32) + matmul(a, dn_t[...].reshape(feat, width))).astype(BF16)
        yb[m] = out
        copy(yb.at[m], xb.at[m], fx, (m,), (s + 1, r)).start()
        pltpu.make_async_copy(yb.at[m], codes_out.at[m], wr.at[m]).start()
        slope = 0.5 * (1.0 + t) + (0.5 * C0) * v * (1.0 - t * t) * (1.0 + (3.0 * C1) * (v * v))
        q[m] = (slope * gain_row[...]).astype(BF16)
        act[m] = a
        wh[1, m] = hidden.astype(BF16)
        sc[m] = jnp.broadcast_to(scale, sc.shape[1:])
        return 0

    pl.when(s == 0)(fetch_codes.wait)
    pl.when(s == last)(fetch_cot.wait)

    @pl.when(s < last)
    def _():
        lax.fori_loop(0, micro, forward, 0)


    def prepare(i, _):
        some = pl.ds(i * (micro // 2), micro // 2)
        rows = micro // 2 * ROWS
        h_b = wh[1, some].reshape(rows, feat)
        product = q[some].reshape(rows, feat).astype(F32) * h_b.astype(F32)
        scale = sc[some].reshape(rows, 128)[:, 0:1]
        kk_f = matmul(product.astype(BF16), dn_t[...].reshape(feat, width)) * (1.0 / feat)
        kk[some] = kk_f.reshape(micro // 2, ROWS, width)
        h2_f = matmul(h_b, up_t[...].reshape(feat, width)) * (scale * scale * scale)
        h2[some] = h2_f.reshape(micro // 2, ROWS, width)
        return 0

    pl.when(s == 0)(transpose_dn)

    @pl.when(s < last)
    def _():
        lax.fori_loop(0, 2, prepare, 0)


    gg_acc[...] = jnp.zeros_like(gg_acc)

    def add_gain(m):
        term = wh[0, m].astype(F32) * (wh[1, m].astype(F32) * sc[m][:, 0:1])
        gg_acc[...] += jnp.sum(term.reshape(ROWS // 8, 8, feat), axis=0)

    half = micro // 2

    def backward(m, _, first):
        arrived(gb.at[m], bg, (m,))
        g = gb[m]
        g_f = g.astype(F32)
        w = (matmul(g, dn_n[...]) * q[m].astype(F32)).astype(BF16)
        mean = jnp.sum(g_f * kk[m], axis=1, keepdims=True)
        scale = sc[m][:, 0:1]
        if not first:
            mixed = matmul(w, up_t[...].reshape(feat, width))
            gi[m] = (g_f + scale * mixed - mean * h2[m]).astype(BF16)
            copy(gi.at[m], gb.at[m], bg, (m,), (s - 1, r)).start()
        wh[0, m] = w
        x = xb[m].astype(F32)
        xs[0, m] = (scale * x).astype(BF16)
        xs[1, m] = (x * (-(scale * scale * scale) * mean)).astype(BF16)

        if first:
            add_gain(m)
        return 0

    @pl.when(s == 0)
    def _():
        lax.fori_loop(0, micro, functools.partial(backward, first=True), 0)

    @pl.when((s > 0) & (s < last))
    def _():
        lax.fori_loop(0, micro, functools.partial(backward, first=False), 0)

    def both(m, _):
        arrived(xb.at[m], fx, (m,))
        x = xb[m]
        hidden = matmul(x, up_n[...])
        scale = lax.rsqrt(jnp.sum(hidden * hidden, axis=1, keepdims=True) * (1.0 / feat) + EPS)
        v = hidden * scale * gain_row[...]
        t = jnp.tanh(C0 * (v + C1 * (v * v * v)))
        act[m] = (0.5 * v * (1.0 + t)).astype(BF16)
        slope = 0.5 * (1.0 + t) + (0.5 * C0) * v * (1.0 - t * t) * (1.0 + (3.0 * C1) * (v * v))
        w = wh[0, m].astype(F32) * (slope * gain_row[...])
        mean = jnp.sum(w * hidden, axis=1, keepdims=True) * (1.0 / feat)
        d_hid = (scale * (w - hidden * (scale * scale * mean))).astype(BF16)
        mixed = matmul(d_hid, up_t[...].reshape(feat, width))
        gi[m] = (gb[m].astype(F32) + mixed).astype(BF16)
        copy(gi.at[m], gb.at[m], bg, (m,), (s - 1, r)).start()
        wh[0, m] = w.astype(BF16)
        wh[1, m] = hidden.astype(BF16)
        sc[m] = jnp.broadcast_to(scale, sc.shape[1:])
        x = x.astype(F32)
        xs[0, m] = (scale * x).astype(BF16)
        xs[1, m] = (x * (-(scale * scale * scale) * mean)).astype(BF16)
        return 0

    @pl.when(s == last)
    def _():
        def ahead(i, _):
            some = pl.ds(i * half, half)
            d_act = matmul(gb[some].reshape(half * ROWS, width), dn_n[...])
            wh[0, some] = d_act.astype(BF16).reshape(half, ROWS, feat)
            return 0

        def after(i, _):
            some = pl.ds(i * half, half)
            a = act[some].reshape(half * ROWS, feat)
            mixed = matmul(a, dn_t[...].reshape(feat, width)).reshape(half, ROWS, width)
            yb[some] = (xb[some].astype(F32) + mixed).astype(BF16)
            for j in range(half):
                m = i * half + j
                pltpu.make_async_copy(yb.at[m], codes_out.at[m], wr.at[m]).start()
            return 0

        lax.fori_loop(0, 2, ahead, 0)
        lax.fori_loop(0, micro, both, 0)
        lax.fori_loop(0, 2, after, 0)

    parts = (part_up, part_dn)
    rz, ry, z2, y2 = (rz_up, rz_dn), (ry_up, ry_dn), (rz2_up, rz2_dn), (ry2_up, ry2_dn)
    outs = (gu_out, gd_out)

    def part_y(a, e, h):
        return parts[a].at[2 * h:2 * h + 2, at_y(e), 0:CUT[a]]

    def part_z(a, d, g):
        return parts[a].at[d % NZ, 4 * g:4 * g + 4, CUT[a]:]

    def add_into(ref, other):
        ref[...] = (ref[...].astype(F32) + other[...].astype(F32)).astype(BF16)

    def ring_step(a, k, halves=(0, 1)):
        for h in halves:
            for side in range(2):
                steps = 4 if h == side else 3
                if k > steps:
                    continue
                ref = part_y(a, (steps - k, k - steps)[side], h)
                if k > 0:
                    got = rz[a].at[side, h, k - 1]
                    arrived(got, rz1, (a, side, h, k - 1))
                    add_into(ref, got)
                if k < steps:
                    send(ref, rz[a].at[side, h, k], rz1, (a, side, h, k), (right, left)[side])

    def line_send(a, side, d, g, cond):
        dst = ry[a].at[side, d - 1, 4 * g:4 * g + 4]
        send(part_z(a, (d, -d)[side], g), dst, ry1, (a, side, d - 1, g), (above, below)[side], cond)

    def line_step(a, d):
        for g in range(2):
            for side in range(2):
                way = (z, NZ - 1 - z)[side]
                got = ry[a].at[side, d, 4 * g:4 * g + 4]

                @pl.when((way >= 1) & (way <= NZ - 1 - d))
                def _():
                    arrived(got, ry1, (a, side, d, g))
                    add_into(part_z(a, (d, -d)[side], g), got)

                if d > 0:
                    line_send(a, side, d, g, way <= NZ - 1 - d)

    tokens = micro * ROWS

    def fill(a, h):
        for i in (2 * h, 2 * h + 1):
            cols = slice(group * i, group * (i + 1))
            if a == 1:
                left = act[:, :, cols].reshape(tokens, group)
                right = gb[...].reshape(tokens, width)
            else:
                left = wh[:, :, :, cols].reshape(2 * tokens, group)
                right = xs[...].reshape(2 * tokens, width)
            parts[a][i] = matmul(left, right, TN).astype(BF16).reshape(part_up.shape[1:])
        ring_step(a, 0, (h,))

    for a in (1, 0):
        fill(a, 0)
        fill(a, 1)
        for side in range(2):
            for g in range(2):
                line_send(a, side, NZ - 1, g, (z == 0, z == NZ - 1)[side])
    ring_step(1, 1)

    @pl.when(s > 0)
    def _():
        def gain_of(m, _):
            add_gain(m)
            return 0

        lax.fori_loop(0, micro, gain_of, 0)

    total = jnp.sum(gg_acc[...], axis=0, keepdims=True) / gain_row[...]
    gg_tot[...] = jnp.zeros_like(gg_tot)
    for d in range(NZ):
        for c in range(group // 128):
            lane = group * d + 128 * c
            gg_tot[0, pl.ds(at_z(d) * (group // 128) + c, 1), :] = total[:, lane:lane + 128]
    for d in range(1, NY):
        send(gg_tot.at[0], gg_y.at[d], hys, (d,), dev(z, at_y(d)))

    ring_step(0, 1)
    line_step(1, 2)
    line_step(0, 2)
    total = gg_tot[0]
    for d in range(1, NY):
        arrived(gg_y.at[d], hys, (d,))
        total = total + gg_y[d]
    gg_tot[1] = total
    for d in range(1, NZ):
        send(gg_tot.at[1], gg_z.at[d], hzs, (d,), dev(at_z(d), y))
    for k in (2, 3):
        for a in (1, 0):
            ring_step(a, k)
        for a in (1, 0):
            line_step(a, 3 - k)

    for a in (1, 0):
        for d in range(1, NY):
            send(parts[a].at[0, at_y(d), CUT[a]:], y2[a].at[d], ry2, (a, d), dev(z, at_y(d)))
    for a in (1, 0):
        kz = CUT[a]
        ring_step(a, 4)
        for d in range(1, NZ):
            send(parts[a].at[d, y, 0:kz], z2[a].at[d], rz2, (a, d), dev(at_z(d), y))
    for a in (1, 0):
        kz = CUT[a]
        total = parts[a][0, y, kz:].astype(F32)
        for d in range(1, NY):
            arrived(y2[a].at[d], ry2, (a, d))
            total = total + y2[a][d].astype(F32)
        outs[a][kz:] = total
    for a in (1, 0):
        kz = CUT[a]
        total = parts[a][0, y, 0:kz].astype(F32)
        for d in range(1, NZ):
            arrived(z2[a].at[d], rz2, (a, d))
            total = total + z2[a][d].astype(F32)
        outs[a][0:kz] = total
    total = gg_tot[1]
    for d in range(1, NZ):
        arrived(gg_z.at[d], hzs, (d,))
        total = total + gg_z[d]
    gg_z[0] = total
    for i in range(8):
        head = min(piece, 128 - 16 * i)

        @pl.when(cut == i)
        def _():
            gg_out[:, 0:head] = gg_z[0, pl.ds(row, 1), 16 * i:16 * i + head]
            if head < piece:
                gg_out[:, head:] = gg_z[0, pl.ds(row + 1, 1), 0:piece - head]


    for c, cond in pending:
        if cond is None:
            c.wait_send()
        else:
            pl.when(cond)(c.wait_send)

    def drain(m, _):
        pltpu.make_async_copy(yb.at[m], codes_out.at[m], wr.at[m]).wait()

        @pl.when(s < last)
        def _():
            copy(yb.at[m], xb.at[m], fx, (m,), (s + 1, r)).wait_send()

        @pl.when(s > 0)
        def _():
            copy(gi.at[m], gb.at[m], bg, (m,), (s - 1, r)).wait_send()

        return 0

    lax.fori_loop(0, micro, drain, 0)


def hand_over(*refs):
    count = len(refs) // 2
    for i in range(count):
        refs[count + i][...] = refs[i][...]


def on_device(codes_in, cotangent, up, down, gain):
    rows, width = codes_in.shape
    piece = up.shape[2]
    feat = piece * lax.axis_size("replica")
    micro = rows // ROWS
    grid = (NZ, NY, piece, width)
    small = (-(-feat // 1024) * 8, 128)

    def vm(shape, dtype=BF16):
        return pltpu.VMEM(shape, dtype)

    def sem(*shape):
        return pltpu.SemaphoreType.DMA((2,) + shape)

    ku, kd = CUT
    scratch = [
        vm(grid), vm(grid), vm((width, feat)), vm((width, feat)), vm((1, feat), F32),
        vm((micro, ROWS, width)), vm((micro, ROWS, width)), vm((micro, ROWS, width)),
        vm((micro, ROWS, feat)), vm((2, micro, ROWS, feat)), vm((micro, ROWS, feat)),
        vm((2, micro, ROWS, width)), vm((micro, ROWS, 128), F32),
        vm((micro, ROWS, width), F32), vm((micro, ROWS, width), F32),
        vm(grid), vm(grid),
        vm((2, 2, 4, 2, ku, width)), vm((2, 2, 4, 2, kd, width)),
        vm((2, NZ, NY, piece - ku, width)), vm((2, NZ, NY, piece - kd, width)),
        vm((NZ, ku, width)), vm((NZ, kd, width)),
        vm((NY, piece - ku, width)), vm((NY, piece - kd, width)),
        vm(small, F32), vm(small, F32), vm((NY,) + small, F32), vm((NZ,) + small, F32),
        vm((8, feat), F32), vm((2,) + small, F32), vm((NY,) + small, F32), vm((NZ,) + small, F32),
        sem(2, NZ), sem(2, 2, 4), sem(2, 2, 2, 4), sem(2, 2, 3), sem(NY), sem(NZ),
        sem(micro), sem(micro),
        sem(2, 2, 2, 4), sem(2, 2, NZ, 2), sem(2, NZ), sem(2, NY), sem(NY), sem(NZ),
        vm((micro, ROWS, width)), pltpu.SemaphoreType.DMA((2,)), pltpu.SemaphoreType.DMA((micro,)),
    ]
    results = pl.pallas_call(
        kernel,
        out_shape=(
            jax.ShapeDtypeStruct((micro, ROWS, width), BF16),
            jax.ShapeDtypeStruct((piece, width), F32),
            jax.ShapeDtypeStruct((piece, width), F32),
            jax.ShapeDtypeStruct((1, piece), F32),
        ),
        in_specs=[pl.BlockSpec(memory_space=pl.ANY)] * 2 + [pl.BlockSpec(memory_space=pltpu.VMEM)] * 3,
        out_specs=(pl.BlockSpec(memory_space=pl.ANY),) + (pl.BlockSpec(memory_space=pltpu.VMEM),) * 3,
        scratch_shapes=scratch,
        compiler_params=pltpu.CompilerParams(
            collective_id=0, has_side_effects=True, vmem_limit_bytes=56 << 20
        ),
    )(codes_in.reshape(micro, ROWS, width), cotangent.reshape(micro, ROWS, width), up[0].T, down[0].T, gain)
    codes, grad_up, grad_dn, grad_gain = pl.pallas_call(
        hand_over,
        out_shape=tuple(jax.ShapeDtypeStruct(x.shape, x.dtype) for x in results),
        in_specs=[pl.BlockSpec(memory_space=pltpu.VMEM)] * len(results),
        out_specs=tuple([pl.BlockSpec(memory_space=pltpu.VMEM)] * len(results)),
    )(*results)
    return (codes.reshape(1, rows, width), grad_up.T[None], grad_dn.T[None], grad_gain)


def solution(mesh):
    placed = (
        P("replica", None),
        P("replica", None),
        P("section", None, "replica"),
        P("section", None, "replica"),
        P("section", "replica"),
    )
    return jax.shard_map(
        on_device,
        mesh=mesh,
        in_specs=placed,
        out_specs=(
            P("section", "replica", None),
            P("section", None, "replica"),
            P("section", None, "replica"),
            P("section", "replica"),
        ),
        check_vma=False,
    )
```

```python
import functools

import jax
import jax.numpy as jnp
from jax import lax
from jax.experimental import pallas as pl
from jax.experimental.pallas import tpu as pltpu
from jax.sharding import PartitionSpec as P

MESH = pl.DeviceIdType.MESH
EPS = 1e-06
NY, NZ = 8, 4
ROWS = 64
SPLIT = (48, 64)
CUT = (48, 48)
SHORT = ((4, 3), (3, 4))
C0 = 0.7978845608028654
C1 = 0.044715
NN = (((1,), (0,)), ((), ()))
TN = (((0,), (0,)), ((), ()))
F32 = jnp.float32
BF16 = jnp.bfloat16


def matmul(a, b, dims=NN):
    return lax.dot_general(a, b, dims, preferred_element_type=F32)


def kernel(
    codes, cot, up_in, dn_in, gain_in,
    codes_out, gu_out, gd_out, gg_out,
    up_t, dn_t, up_n, dn_n, gain_row,
    xb, gb, gi, act, wh, q, xs, sc, kk, h2,
    part_up, part_dn, rz_up, rz_dn, ry_up, ry_dn, rz2_up, rz2_dn, ry2_up, ry2_dn,
    gain_own, gain_tot, gain_y, gain_z, gg_acc, gg_tot, gg_y, gg_z,
    zp1, yp1, zp2, yp2, gys, gzs, fx, bg, rz1, ry1, rz2, ry2, hys, hzs, yb, io, wr,
):
    last = lax.axis_size("section") - 1
    s = lax.axis_index("section")
    r = lax.axis_index("replica")
    y = lax.rem(r, NY)
    z = r // NY
    micro = xb.shape[0]
    feat = gain_row.shape[1]
    width = xb.shape[2]

    def at_y(d):
        return lax.rem(y + d + NY, NY)

    def at_z(d):
        return lax.rem(z + d + NZ, NZ)

    def dev(z_, y_):
        return (s, z_ * NY + y_)

    pending = []

    def copy(src, dst, sems, index, to):
        return pltpu.make_async_remote_copy(
            src_ref=src, dst_ref=dst,
            send_sem=sems.at[(0,) + index], recv_sem=sems.at[(1,) + index],
            device_id=to, device_id_type=MESH,
        )

    def send(src, dst, sems, index, to, cond=None):
        c = copy(src, dst, sems, index, to)
        if cond is None:
            c.start()
        else:
            pl.when(cond)(c.start)
        pending.append((c, cond))

    def arrived(dst, sems, index, cond=None):
        c = copy(dst, dst, sems, index, (s, r))
        if cond is None:
            c.wait_recv()
        else:
            pl.when(cond)(c.wait_recv)

    fetch_codes = pltpu.make_async_copy(codes, xb, io.at[0])
    fetch_cot = pltpu.make_async_copy(cot, gb, io.at[1])
    pl.when(s == 0)(fetch_codes.start)
    pl.when(s == last)(fetch_cot.start)

    barrier = pltpu.get_barrier_semaphore()
    for d in range(1, NY):
        pl.semaphore_signal(barrier, inc=1, device_id=dev(z, at_y(d)), device_id_type=MESH)
    for d in range(1, NZ):
        pl.semaphore_signal(barrier, inc=1, device_id=dev(at_z(d), y), device_id_type=MESH)

    @pl.when(s > 0)
    def _():
        pl.semaphore_signal(barrier, inc=1, device_id=(s - 1, r), device_id_type=MESH)

    @pl.when(s < last)
    def _():
        pl.semaphore_signal(barrier, inc=1, device_id=(s + 1, r), device_id_type=MESH)

    full = (up_t, dn_t)
    for a in range(2):
        full[a][0, y] = (up_in, dn_in)[a][...]

    row, cut = (5 * r) // 8, lax.rem(5 * r, 8)
    gain_own[...] = jnp.zeros_like(gain_own)
    piece = up_in.shape[0]
    for i in range(8):
        head = min(piece, 128 - 16 * i)

        @pl.when(cut == i)
        def _():
            gain = gain_in[...].astype(F32)
            gain_own[pl.ds(row, 1), 16 * i:16 * i + head] = gain[:, :head]
            if head < piece:
                gain_own[pl.ds(row + 1, 1), 0:piece - head] = gain[:, head:]

    pl.semaphore_wait(
        barrier, NY - 1 + NZ - 1 + jnp.where(s > 0, 1, 0) + jnp.where(s < last, 1, 0)
    )

    def block_y(a, e, part=slice(0, NZ)):
        return full[a].at[part, at_y(e), 0:SPLIT[a]]

    def block_z(a, d):
        return full[a].at[d % NZ, :, SPLIT[a]:]

    right, left = dev(z, at_y(1)), dev(z, at_y(-1))
    above, below = dev(jnp.minimum(z + 1, NZ - 1), y), dev(jnp.maximum(z - 1, 0), y)
    first = (slice(0, 1), slice(0, 1))
    rest = (slice(1, NZ), slice(1, NZ))

    def ring(a, stream, side, k):
        if k < 3:
            return (first, rest)[stream][side]
        return ((slice(0, 1), None), (slice(1, 2), slice(2, NZ)))[stream][side]

    def ring_send(a, stream, side, k):
        part = ring(a, stream, side, k)
        if part is not None:
            e = (-k, k)[side]
            send(block_y(a, e, part), block_y(a, e, part), zp2, (a, stream, side, k), (right, left)[side])

    def short_send(a, side, k):
        if k < SHORT[a][side]:
            ref = full[a].at[0, at_y((-k, k)[side]), SPLIT[a]:]
            send(ref, ref, yp1, (a, side, k), (right, left)[side])

    def short_wait(a, side, k):
        if k < SHORT[a][side]:
            ref = full[a].at[0, at_y((-k - 1, k + 1)[side]), SPLIT[a]:]
            arrived(ref, yp1, (a, side, k))

    def ring_wait(a, stream, side, k):
        part = ring(a, stream, side, k)
        if part is not None:
            arrived(block_y(a, (-k - 1, k + 1)[side], part), zp2, (a, stream, side, k))

    for a in range(2):
        for side in range(2):
            short_send(a, side, 0)
    for a in range(2):
        kz = SPLIT[a]
        for d in range(1, NZ):
            send(full[a].at[0, y, 0:kz], full[a].at[NZ - d, y, 0:kz], zp1, (a, d), dev(at_z(d), y))
        for side in range(2):
            ring_send(a, 0, side, 0)
    for d in range(1, NY):
        send(gain_own, gain_y.at[d], gys, (d,), dev(z, at_y(d)))

    def short_step(k):
        for a in range(2):
            for side in range(2):
                short_wait(a, side, k - 1)
                short_send(a, side, k)

    short_step(1)
    short_step(2)
    for a in range(2):
        for d in range(1, NZ):
            arrived(full[a].at[NZ - d, y, 0:SPLIT[a]], zp1, (a, d))
        for side in range(2):
            ring_send(a, 1, side, 0)
    short_step(3)
    short_step(4)
    for a in range(2):
        send(block_z(a, 0), block_z(a, -1), yp2, (a, 0, 0), above, z < NZ - 1)
        send(block_z(a, 0), block_z(a, 1), yp2, (a, 1, 0), below, z > 0)
    total = gain_own[...]
    for d in range(1, NY):
        arrived(gain_y.at[d], gys, (d,))
        total = total + gain_y[d]
    gain_tot[...] = total
    for d in range(1, NZ):
        send(gain_tot, gain_z.at[d], gzs, (d,), dev(at_z(d), y))
    for k in range(1, 4):
        for stream in range(2):
            for a in range(2):
                for side in range(2):
                    ring_wait(a, stream, side, k - 1)
                    ring_send(a, stream, side, k)
        for a in range(2):
            arrived(block_z(a, -k), yp2, (a, 0, k - 1), z >= k)
            if k < 3:
                send(block_z(a, -k), block_z(a, -k - 1), yp2, (a, 0, k), above, (z >= k) & (z < NZ - 1))
            arrived(block_z(a, k), yp2, (a, 1, k - 1), z <= NZ - 1 - k)
            if k < 3:
                send(block_z(a, k), block_z(a, k + 1), yp2, (a, 1, k), below, (z <= NZ - 1 - k) & (z > 0))
    for stream in range(2):
        for side in range(2):
            ring_wait(0, stream, side, 3)
    total = gain_tot[...]
    for d in range(1, NZ):
        arrived(gain_z.at[d], gzs, (d,))
        total = total + gain_z[d]
    gain_z[0] = total
    group = feat // NZ
    for d in range(NZ):
        for c in range(group // 128):
            lane = group * d + 128 * c
            gain_row[:, lane:lane + 128] = gain_z[0, pl.ds(at_z(d) * (group // 128) + c, 1), :]

    for i in range(NZ):
        up_n[:, group * i:group * (i + 1)] = up_t[i].reshape(group, width).T
    for stream in range(2):
        for side in range(2):
            ring_wait(1, stream, side, 3)

    def transpose_dn():
        for i in range(NZ):
            dn_n[:, group * i:group * (i + 1)] = dn_t[i].reshape(group, width).T

    pl.when(s > 0)(transpose_dn)

    def forward(m, _):
        @pl.when(s > 0)
        def _():
            arrived(xb.at[m], fx, (m,))

        x = xb[m]
        hidden = matmul(x, up_n[...])
        scale = lax.rsqrt(jnp.sum(hidden * hidden, axis=1, keepdims=True) * (1.0 / feat) + EPS)
        v = hidden * scale * gain_row[...]
        v2 = v * v
        t = jnp.tanh(v * (C0 + (C0 * C1) * v2))
        half_v = 0.5 * v
        a = (half_v + half_v * t).astype(BF16)
        out = (x.astype(F32) + matmul(a, dn_t[...].reshape(feat, width))).astype(BF16)
        yb[m] = out
        copy(yb.at[m], xb.at[m], fx, (m,), (s + 1, r)).start()
        pltpu.make_async_copy(yb.at[m], codes_out.at[m], wr.at[m]).start()
        slope = (0.5 + 0.5 * t) + half_v * (1.0 - t * t) * (C0 + (3.0 * C0 * C1) * v2)
        q[m] = (slope * gain_row[...]).astype(BF16)
        act[m] = a
        wh[1, m] = hidden.astype(BF16)
        sc[m] = jnp.broadcast_to(scale, sc.shape[1:])
        return 0

    pl.when(s == 0)(fetch_codes.wait)
    pl.when(s == last)(fetch_cot.wait)

    @pl.when(s < last)
    def _():
        lax.fori_loop(0, micro, forward, 0)


    def prepare(i, _):
        some = pl.ds(i * (micro // 2), micro // 2)
        rows = micro // 2 * ROWS
        h_b = wh[1, some].reshape(rows, feat)
        product = q[some].reshape(rows, feat).astype(F32) * h_b.astype(F32)
        scale = sc[some].reshape(rows, 128)[:, 0:1]
        kk_f = matmul(product.astype(BF16), dn_t[...].reshape(feat, width)) * (1.0 / feat)
        kk[some] = kk_f.reshape(micro // 2, ROWS, width)
        h2_f = matmul(h_b, up_t[...].reshape(feat, width)) * (scale * scale * scale)
        h2[some] = h2_f.reshape(micro // 2, ROWS, width)
        return 0

    pl.when(s == 0)(transpose_dn)

    @pl.when(s < last)
    def _():
        lax.fori_loop(0, 2, prepare, 0)


    gg_acc[...] = jnp.zeros_like(gg_acc)

    def add_gain(m):
        term = wh[0, m].astype(F32) * (wh[1, m].astype(F32) * sc[m][:, 0:1])
        gg_acc[...] += jnp.sum(term.reshape(ROWS // 8, 8, feat), axis=0)

    half = micro // 2

    def backward(m, _, first):
        arrived(gb.at[m], bg, (m,))
        g = gb[m]
        g_f = g.astype(F32)
        w = (matmul(g, dn_n[...]) * q[m].astype(F32)).astype(BF16)
        mean = jnp.sum(g_f * kk[m], axis=1, keepdims=True)
        scale = sc[m][:, 0:1]
        if not first:
            mixed = matmul(w, up_t[...].reshape(feat, width))
            gi[m] = (g_f + scale * mixed - mean * h2[m]).astype(BF16)
            copy(gi.at[m], gb.at[m], bg, (m,), (s - 1, r)).start()
        wh[0, m] = w
        x = xb[m].astype(F32)
        xs[0, m] = (scale * x).astype(BF16)
        xs[1, m] = (x * (-(scale * scale * scale) * mean)).astype(BF16)

        if first:
            add_gain(m)
        return 0

    @pl.when(s == 0)
    def _():
        lax.fori_loop(0, micro, functools.partial(backward, first=True), 0)

    @pl.when((s > 0) & (s < last))
    def _():
        lax.fori_loop(0, micro, functools.partial(backward, first=False), 0)

    def both(m, _):
        arrived(xb.at[m], fx, (m,))
        x = xb[m]
        hidden = matmul(x, up_n[...])
        scale = lax.rsqrt(jnp.sum(hidden * hidden, axis=1, keepdims=True) * (1.0 / feat) + EPS)
        v = hidden * scale * gain_row[...]
        v2 = v * v
        t = jnp.tanh(v * (C0 + (C0 * C1) * v2))
        half_v = 0.5 * v
        act[m] = (half_v + half_v * t).astype(BF16)
        slope = (0.5 + 0.5 * t) + half_v * (1.0 - t * t) * (C0 + (3.0 * C0 * C1) * v2)
        w = wh[0, m].astype(F32) * (slope * gain_row[...])
        mean = jnp.sum(w * hidden, axis=1, keepdims=True) * (1.0 / feat)
        d_hid = (scale * (w - hidden * (scale * scale * mean))).astype(BF16)
        mixed = matmul(d_hid, up_t[...].reshape(feat, width))
        gi[m] = (gb[m].astype(F32) + mixed).astype(BF16)
        copy(gi.at[m], gb.at[m], bg, (m,), (s - 1, r)).start()
        wh[0, m] = w.astype(BF16)
        wh[1, m] = hidden.astype(BF16)
        sc[m] = jnp.broadcast_to(scale, sc.shape[1:])
        x = x.astype(F32)
        xs[0, m] = (scale * x).astype(BF16)
        xs[1, m] = (x * (-(scale * scale * scale) * mean)).astype(BF16)
        return 0

    @pl.when(s == last)
    def _():
        def ahead(i, _):
            some = pl.ds(i * half, half)
            d_act = matmul(gb[some].reshape(half * ROWS, width), dn_n[...])
            wh[0, some] = d_act.astype(BF16).reshape(half, ROWS, feat)
            return 0

        def after(i, _):
            some = pl.ds(i * half, half)
            a = act[some].reshape(half * ROWS, feat)
            mixed = matmul(a, dn_t[...].reshape(feat, width)).reshape(half, ROWS, width)
            yb[some] = (xb[some].astype(F32) + mixed).astype(BF16)
            for j in range(half):
                m = i * half + j
                pltpu.make_async_copy(yb.at[m], codes_out.at[m], wr.at[m]).start()
            return 0

        lax.fori_loop(0, 2, ahead, 0)
        lax.fori_loop(0, micro, both, 0)
        lax.fori_loop(0, 2, after, 0)

    parts = (part_up, part_dn)
    rz, ry, z2, y2 = (rz_up, rz_dn), (ry_up, ry_dn), (rz2_up, rz2_dn), (ry2_up, ry2_dn)
    outs = (gu_out, gd_out)

    def part_y(a, e, h):
        return parts[a].at[2 * h:2 * h + 2, at_y(e), 0:CUT[a]]

    def part_z(a, d, g):
        return parts[a].at[d % NZ, 4 * g:4 * g + 4, CUT[a]:]

    def add_into(ref, other):
        ref[...] = (ref[...].astype(F32) + other[...].astype(F32)).astype(BF16)

    def ring_step(a, k, halves=(0, 1)):
        for h in halves:
            for side in range(2):
                steps = 4 if h == side else 3
                if k > steps:
                    continue
                ref = part_y(a, (steps - k, k - steps)[side], h)
                if k > 0:
                    got = rz[a].at[side, h, k - 1]
                    arrived(got, rz1, (a, side, h, k - 1))
                    add_into(ref, got)
                if k < steps:
                    send(ref, rz[a].at[side, h, k], rz1, (a, side, h, k), (right, left)[side])

    def line_send(a, side, d, g, cond):
        dst = ry[a].at[side, d - 1, 4 * g:4 * g + 4]
        send(part_z(a, (d, -d)[side], g), dst, ry1, (a, side, d - 1, g), (above, below)[side], cond)

    def line_step(a, d):
        for g in range(2):
            for side in range(2):
                way = (z, NZ - 1 - z)[side]
                got = ry[a].at[side, d, 4 * g:4 * g + 4]

                @pl.when((way >= 1) & (way <= NZ - 1 - d))
                def _():
                    arrived(got, ry1, (a, side, d, g))
                    add_into(part_z(a, (d, -d)[side], g), got)

                if d > 0:
                    line_send(a, side, d, g, way <= NZ - 1 - d)

    tokens = micro * ROWS

    def fill(a, h):
        for i in (2 * h, 2 * h + 1):
            cols = slice(group * i, group * (i + 1))
            if a == 1:
                left = act[:, :, cols].reshape(tokens, group)
                right = gb[...].reshape(tokens, width)
            else:
                left = wh[:, :, :, cols].reshape(2 * tokens, group)
                right = xs[...].reshape(2 * tokens, width)
            parts[a][i] = matmul(left, right, TN).astype(BF16).reshape(part_up.shape[1:])
        ring_step(a, 0, (h,))

    for a in (1, 0):
        fill(a, 0)
        fill(a, 1)
        for side in range(2):
            for g in range(2):
                line_send(a, side, NZ - 1, g, (z == 0, z == NZ - 1)[side])
    ring_step(1, 1)

    @pl.when(s > 0)
    def _():
        def gain_of(m, _):
            add_gain(m)
            return 0

        lax.fori_loop(0, micro, gain_of, 0)

    total = jnp.sum(gg_acc[...], axis=0, keepdims=True) / gain_row[...]
    gg_tot[...] = jnp.zeros_like(gg_tot)
    for d in range(NZ):
        for c in range(group // 128):
            lane = group * d + 128 * c
            gg_tot[0, pl.ds(at_z(d) * (group // 128) + c, 1), :] = total[:, lane:lane + 128]
    for d in range(1, NY):
        send(gg_tot.at[0], gg_y.at[d], hys, (d,), dev(z, at_y(d)))

    ring_step(0, 1)
    line_step(1, 2)
    line_step(0, 2)
    total = gg_tot[0]
    for d in range(1, NY):
        arrived(gg_y.at[d], hys, (d,))
        total = total + gg_y[d]
    gg_tot[1] = total
    for d in range(1, NZ):
        send(gg_tot.at[1], gg_z.at[d], hzs, (d,), dev(at_z(d), y))
    for k in (2, 3):
        for a in (1, 0):
            ring_step(a, k)
        for a in (1, 0):
            line_step(a, 3 - k)

    for a in (1, 0):
        for d in range(1, NY):
            send(parts[a].at[0, at_y(d), CUT[a]:], y2[a].at[d], ry2, (a, d), dev(z, at_y(d)))
    for a in (1, 0):
        kz = CUT[a]
        ring_step(a, 4)
        for d in range(1, NZ):
            send(parts[a].at[d, y, 0:kz], z2[a].at[d], rz2, (a, d), dev(at_z(d), y))
    for a in (1, 0):
        kz = CUT[a]
        total = parts[a][0, y, kz:].astype(F32)
        for d in range(1, NY):
            arrived(y2[a].at[d], ry2, (a, d))
            total = total + y2[a][d].astype(F32)
        outs[a][kz:] = total
    for a in (1, 0):
        kz = CUT[a]
        total = parts[a][0, y, 0:kz].astype(F32)
        for d in range(1, NZ):
            arrived(z2[a].at[d], rz2, (a, d))
            total = total + z2[a][d].astype(F32)
        outs[a][0:kz] = total
    total = gg_tot[1]
    for d in range(1, NZ):
        arrived(gg_z.at[d], hzs, (d,))
        total = total + gg_z[d]
    gg_z[0] = total
    for i in range(8):
        head = min(piece, 128 - 16 * i)

        @pl.when(cut == i)
        def _():
            gg_out[:, 0:head] = gg_z[0, pl.ds(row, 1), 16 * i:16 * i + head]
            if head < piece:
                gg_out[:, head:] = gg_z[0, pl.ds(row + 1, 1), 0:piece - head]


    for c, cond in pending:
        if cond is None:
            c.wait_send()
        else:
            pl.when(cond)(c.wait_send)

    def drain(m, _):
        pltpu.make_async_copy(yb.at[m], codes_out.at[m], wr.at[m]).wait()

        @pl.when(s < last)
        def _():
            copy(yb.at[m], xb.at[m], fx, (m,), (s + 1, r)).wait_send()

        @pl.when(s > 0)
        def _():
            copy(gi.at[m], gb.at[m], bg, (m,), (s - 1, r)).wait_send()

        return 0

    lax.fori_loop(0, micro, drain, 0)


def hand_over(*refs):
    count = len(refs) // 2
    for i in range(count):
        refs[count + i][...] = refs[i][...]


def on_device(codes_in, cotangent, up, down, gain):
    rows, width = codes_in.shape
    piece = up.shape[2]
    feat = piece * lax.axis_size("replica")
    micro = rows // ROWS
    grid = (NZ, NY, piece, width)
    small = (-(-feat // 1024) * 8, 128)

    def vm(shape, dtype=BF16):
        return pltpu.VMEM(shape, dtype)

    def sem(*shape):
        return pltpu.SemaphoreType.DMA((2,) + shape)

    ku, kd = CUT
    scratch = [
        vm(grid), vm(grid), vm((width, feat)), vm((width, feat)), vm((1, feat), F32),
        vm((micro, ROWS, width)), vm((micro, ROWS, width)), vm((micro, ROWS, width)),
        vm((micro, ROWS, feat)), vm((2, micro, ROWS, feat)), vm((micro, ROWS, feat)),
        vm((2, micro, ROWS, width)), vm((micro, ROWS, 128), F32),
        vm((micro, ROWS, width), F32), vm((micro, ROWS, width), F32),
        vm(grid), vm(grid),
        vm((2, 2, 4, 2, ku, width)), vm((2, 2, 4, 2, kd, width)),
        vm((2, NZ, NY, piece - ku, width)), vm((2, NZ, NY, piece - kd, width)),
        vm((NZ, ku, width)), vm((NZ, kd, width)),
        vm((NY, piece - ku, width)), vm((NY, piece - kd, width)),
        vm(small, F32), vm(small, F32), vm((NY,) + small, F32), vm((NZ,) + small, F32),
        vm((8, feat), F32), vm((2,) + small, F32), vm((NY,) + small, F32), vm((NZ,) + small, F32),
        sem(2, NZ), sem(2, 2, 4), sem(2, 2, 2, 4), sem(2, 2, 3), sem(NY), sem(NZ),
        sem(micro), sem(micro),
        sem(2, 2, 2, 4), sem(2, 2, NZ, 2), sem(2, NZ), sem(2, NY), sem(NY), sem(NZ),
        vm((micro, ROWS, width)), pltpu.SemaphoreType.DMA((2,)), pltpu.SemaphoreType.DMA((micro,)),
    ]
    results = pl.pallas_call(
        kernel,
        out_shape=(
            jax.ShapeDtypeStruct((micro, ROWS, width), BF16),
            jax.ShapeDtypeStruct((piece, width), F32),
            jax.ShapeDtypeStruct((piece, width), F32),
            jax.ShapeDtypeStruct((1, piece), F32),
        ),
        in_specs=[pl.BlockSpec(memory_space=pl.ANY)] * 2 + [pl.BlockSpec(memory_space=pltpu.VMEM)] * 3,
        out_specs=(pl.BlockSpec(memory_space=pl.ANY),) + (pl.BlockSpec(memory_space=pltpu.VMEM),) * 3,
        scratch_shapes=scratch,
        compiler_params=pltpu.CompilerParams(
            collective_id=0, has_side_effects=True, vmem_limit_bytes=56 << 20
        ),
    )(codes_in.reshape(micro, ROWS, width), cotangent.reshape(micro, ROWS, width), up[0].T, down[0].T, gain)
    codes, grad_up, grad_dn, grad_gain = pl.pallas_call(
        hand_over,
        out_shape=tuple(jax.ShapeDtypeStruct(x.shape, x.dtype) for x in results),
        in_specs=[pl.BlockSpec(memory_space=pltpu.VMEM)] * len(results),
        out_specs=tuple([pl.BlockSpec(memory_space=pltpu.VMEM)] * len(results)),
    )(*results)
    return (codes.reshape(1, rows, width), grad_up.T[None], grad_dn.T[None], grad_gain)


def solution(mesh):
    placed = (
        P("replica", None),
        P("replica", None),
        P("section", None, "replica"),
        P("section", None, "replica"),
        P("section", "replica"),
    )
    return jax.shard_map(
        on_device,
        mesh=mesh,
        in_specs=placed,
        out_specs=(
            P("section", "replica", None),
            P("section", None, "replica"),
            P("section", None, "replica"),
            P("section", "replica"),
        ),
        check_vma=False,
    )
```

```python
import functools

import jax
import jax.numpy as jnp
from jax import lax
from jax.experimental import pallas as pl
from jax.experimental.pallas import tpu as pltpu
from jax.sharding import PartitionSpec as P

MESH = pl.DeviceIdType.MESH
EPS = 1e-06
NY, NZ = 8, 4
ROWS = 64
SPLIT = (48, 64)
CUT = (48, 48)
SHORT = ((4, 3), (3, 4))
C0 = 0.7978845608028654
C1 = 0.044715
NN = (((1,), (0,)), ((), ()))
TN = (((0,), (0,)), ((), ()))
F32 = jnp.float32
BF16 = jnp.bfloat16


def matmul(a, b, dims=NN):
    return lax.dot_general(a, b, dims, preferred_element_type=F32)


def kernel(
    codes, cot, up_in, dn_in, gain_in,
    codes_out, gu_out, gd_out, gg_out,
    up_t, dn_t, up_n, dn_n, gain_row,
    xb, gb, gi, act, wh, q, xs, sc, kk, h2,
    part_up, part_dn, rz_up, rz_dn, ry_up, ry_dn, rz2_up, rz2_dn, ry2_up, ry2_dn,
    gain_own, gain_tot, gain_y, gain_z, gg_acc, gg_tot, gg_y, gg_z,
    zp1, yp1, zp2, yp2, gys, gzs, fx, bg, rz1, ry1, rz2, ry2, hys, hzs, yb, io, wr,
):
    last = lax.axis_size("section") - 1
    s = lax.axis_index("section")
    r = lax.axis_index("replica")
    y = lax.rem(r, NY)
    z = r // NY
    micro = xb.shape[0]
    feat = gain_row.shape[1]
    width = xb.shape[2]

    def at_y(d):
        return lax.rem(y + d + NY, NY)

    def at_z(d):
        return lax.rem(z + d + NZ, NZ)

    def dev(z_, y_):
        return (s, z_ * NY + y_)

    pending = []

    def copy(src, dst, sems, index, to):
        return pltpu.make_async_remote_copy(
            src_ref=src, dst_ref=dst,
            send_sem=sems.at[(0,) + index], recv_sem=sems.at[(1,) + index],
            device_id=to, device_id_type=MESH,
        )

    def send(src, dst, sems, index, to, cond=None):
        c = copy(src, dst, sems, index, to)
        if cond is None:
            c.start()
        else:
            pl.when(cond)(c.start)
        pending.append((c, cond))

    def arrived(dst, sems, index, cond=None):
        c = copy(dst, dst, sems, index, (s, r))
        if cond is None:
            c.wait_recv()
        else:
            pl.when(cond)(c.wait_recv)

    fetch_codes = pltpu.make_async_copy(codes, xb, io.at[0])
    fetch_cot = pltpu.make_async_copy(cot, gb, io.at[1])
    pl.when(s == 0)(fetch_codes.start)
    pl.when(s == last)(fetch_cot.start)

    barrier = pltpu.get_barrier_semaphore()
    for d in range(1, NY):
        pl.semaphore_signal(barrier, inc=1, device_id=dev(z, at_y(d)), device_id_type=MESH)
    for d in range(1, NZ):
        pl.semaphore_signal(barrier, inc=1, device_id=dev(at_z(d), y), device_id_type=MESH)

    @pl.when(s > 0)
    def _():
        pl.semaphore_signal(barrier, inc=1, device_id=(s - 1, r), device_id_type=MESH)

    @pl.when(s < last)
    def _():
        pl.semaphore_signal(barrier, inc=1, device_id=(s + 1, r), device_id_type=MESH)

    full = (up_t, dn_t)
    for a in range(2):
        full[a][0, y] = (up_in, dn_in)[a][...]

    row, cut = (5 * r) // 8, lax.rem(5 * r, 8)
    gain_own[...] = jnp.zeros_like(gain_own)
    piece = up_in.shape[0]
    for i in range(8):
        head = min(piece, 128 - 16 * i)

        @pl.when(cut == i)
        def _():
            gain = gain_in[...].astype(F32)
            gain_own[pl.ds(row, 1), 16 * i:16 * i + head] = gain[:, :head]
            if head < piece:
                gain_own[pl.ds(row + 1, 1), 0:piece - head] = gain[:, head:]

    pl.semaphore_wait(
        barrier, NY - 1 + NZ - 1 + jnp.where(s > 0, 1, 0) + jnp.where(s < last, 1, 0)
    )

    def block_y(a, e, part=slice(0, NZ)):
        return full[a].at[part, at_y(e), 0:SPLIT[a]]

    def block_z(a, d):
        return full[a].at[d % NZ, :, SPLIT[a]:]

    right, left = dev(z, at_y(1)), dev(z, at_y(-1))
    above, below = dev(jnp.minimum(z + 1, NZ - 1), y), dev(jnp.maximum(z - 1, 0), y)
    first = (slice(0, 1), slice(0, 1))
    rest = (slice(1, NZ), slice(1, NZ))

    def ring(a, stream, side, k):
        if k < 3:
            return (first, rest)[stream][side]
        return ((slice(0, 1), None), (slice(1, 2), slice(2, NZ)))[stream][side]

    def ring_send(a, stream, side, k):
        part = ring(a, stream, side, k)
        if part is not None:
            e = (-k, k)[side]
            send(block_y(a, e, part), block_y(a, e, part), zp2, (a, stream, side, k), (right, left)[side])

    def short_send(a, side, k):
        if k < SHORT[a][side]:
            ref = full[a].at[0, at_y((-k, k)[side]), SPLIT[a]:]
            send(ref, ref, yp1, (a, side, k), (right, left)[side])

    def short_wait(a, side, k):
        if k < SHORT[a][side]:
            ref = full[a].at[0, at_y((-k - 1, k + 1)[side]), SPLIT[a]:]
            arrived(ref, yp1, (a, side, k))

    def ring_wait(a, stream, side, k):
        part = ring(a, stream, side, k)
        if part is not None:
            arrived(block_y(a, (-k - 1, k + 1)[side], part), zp2, (a, stream, side, k))

    for a in range(2):
        for side in range(2):
            short_send(a, side, 0)
    for a in range(2):
        kz = SPLIT[a]
        for d in range(1, NZ):
            send(full[a].at[0, y, 0:kz], full[a].at[NZ - d, y, 0:kz], zp1, (a, d), dev(at_z(d), y))
        for side in range(2):
            ring_send(a, 0, side, 0)
    for d in range(1, NY):
        send(gain_own, gain_y.at[d], gys, (d,), dev(z, at_y(d)))

    def short_step(k):
        for a in range(2):
            for side in range(2):
                short_wait(a, side, k - 1)
                short_send(a, side, k)

    short_step(1)
    short_step(2)
    for a in range(2):
        for d in range(1, NZ):
            arrived(full[a].at[NZ - d, y, 0:SPLIT[a]], zp1, (a, d))
        for side in range(2):
            ring_send(a, 1, side, 0)
    short_step(3)
    short_step(4)
    for a in range(2):
        send(block_z(a, 0), block_z(a, -1), yp2, (a, 0, 0), above, z < NZ - 1)
        send(block_z(a, 0), block_z(a, 1), yp2, (a, 1, 0), below, z > 0)
    total = gain_own[...]
    for d in range(1, NY):
        arrived(gain_y.at[d], gys, (d,))
        total = total + gain_y[d]
    gain_tot[...] = total
    for d in range(1, NZ):
        send(gain_tot, gain_z.at[d], gzs, (d,), dev(at_z(d), y))
    for k in range(1, 4):
        for stream in range(2):
            for a in range(2):
                for side in range(2):
                    ring_wait(a, stream, side, k - 1)
                    ring_send(a, stream, side, k)
        for a in range(2):
            arrived(block_z(a, -k), yp2, (a, 0, k - 1), z >= k)
            if k < 3:
                send(block_z(a, -k), block_z(a, -k - 1), yp2, (a, 0, k), above, (z >= k) & (z < NZ - 1))
            arrived(block_z(a, k), yp2, (a, 1, k - 1), z <= NZ - 1 - k)
            if k < 3:
                send(block_z(a, k), block_z(a, k + 1), yp2, (a, 1, k), below, (z <= NZ - 1 - k) & (z > 0))
    for stream in range(2):
        for side in range(2):
            ring_wait(0, stream, side, 3)
    total = gain_tot[...]
    for d in range(1, NZ):
        arrived(gain_z.at[d], gzs, (d,))
        total = total + gain_z[d]
    gain_z[0] = total
    group = feat // NZ
    for d in range(NZ):
        for c in range(group // 128):
            lane = group * d + 128 * c
            gain_row[:, lane:lane + 128] = gain_z[0, pl.ds(at_z(d) * (group // 128) + c, 1), :]

    for i in range(NZ):
        up_n[:, group * i:group * (i + 1)] = up_t[i].reshape(group, width).T
    for stream in range(2):
        for side in range(2):
            ring_wait(1, stream, side, 3)

    def transpose_dn():
        for i in range(NZ):
            dn_n[:, group * i:group * (i + 1)] = dn_t[i].reshape(group, width).T

    pl.when(s > 0)(transpose_dn)

    def forward(m, _):
        @pl.when(s > 0)
        def _():
            arrived(xb.at[m], fx, (m,))

        x = xb[m]
        hidden = matmul(x, up_n[...])
        scale = lax.rsqrt(jnp.sum(hidden * hidden, axis=1, keepdims=True) * (1.0 / feat) + EPS)
        v = hidden * scale * gain_row[...]
        v2 = v * v
        t = jnp.tanh(v * (C0 + (C0 * C1) * v2))
        half_v = 0.5 * v
        a = (half_v + half_v * t).astype(BF16)
        out = (x.astype(F32) + matmul(a, dn_t[...].reshape(feat, width))).astype(BF16)
        yb[m] = out
        copy(yb.at[m], xb.at[m], fx, (m,), (s + 1, r)).start()
        pltpu.make_async_copy(yb.at[m], codes_out.at[m], wr.at[m]).start()
        slope = (0.5 + 0.5 * t) + half_v * (1.0 - t * t) * (C0 + (3.0 * C0 * C1) * v2)
        q[m] = (slope * gain_row[...]).astype(BF16)
        act[m] = a
        wh[1, m] = hidden.astype(BF16)
        sc[m] = jnp.broadcast_to(scale, sc.shape[1:])
        return 0

    pl.when(s == 0)(fetch_codes.wait)
    pl.when(s == last)(fetch_cot.wait)

    @pl.when(s < last)
    def _():
        lax.fori_loop(0, micro, forward, 0)


    def prepare(i, _):
        some = pl.ds(i * (micro // 2), micro // 2)
        rows = micro // 2 * ROWS
        h_b = wh[1, some].reshape(rows, feat)
        product = q[some].reshape(rows, feat).astype(F32) * h_b.astype(F32)
        scale = sc[some].reshape(rows, 128)[:, 0:1]
        kk_f = matmul(product.astype(BF16), dn_t[...].reshape(feat, width)) * (1.0 / feat)
        kk[some] = kk_f.reshape(micro // 2, ROWS, width)
        h2_f = matmul(h_b, up_t[...].reshape(feat, width)) * (scale * scale * scale)
        h2[some] = h2_f.reshape(micro // 2, ROWS, width)
        return 0

    pl.when(s == 0)(transpose_dn)

    @pl.when(s < last)
    def _():
        lax.fori_loop(0, 2, prepare, 0)


    gg_acc[...] = jnp.zeros_like(gg_acc)

    def add_gain(m):
        term = wh[0, m].astype(F32) * (wh[1, m].astype(F32) * sc[m][:, 0:1])
        gg_acc[...] += jnp.sum(term.reshape(ROWS // 8, 8, feat), axis=0)

    half = micro // 2

    def backward(m, _, first):
        arrived(gb.at[m], bg, (m,))
        g = gb[m]
        g_f = g.astype(F32)
        w = (matmul(g, dn_n[...]) * q[m].astype(F32)).astype(BF16)
        mean = jnp.sum(g_f * kk[m], axis=1, keepdims=True)
        scale = sc[m][:, 0:1]
        if not first:
            mixed = matmul(w, up_t[...].reshape(feat, width))
            gi[m] = (g_f + scale * mixed - mean * h2[m]).astype(BF16)
            copy(gi.at[m], gb.at[m], bg, (m,), (s - 1, r)).start()
        wh[0, m] = w
        x = xb[m].astype(F32)
        xs[0, m] = (scale * x).astype(BF16)
        xs[1, m] = (x * (-(scale * scale * scale) * mean)).astype(BF16)

        if first:
            add_gain(m)
        return 0

    @pl.when(s == 0)
    def _():
        lax.fori_loop(0, micro, functools.partial(backward, first=True), 0)

    @pl.when((s > 0) & (s < last))
    def _():
        lax.fori_loop(0, micro, functools.partial(backward, first=False), 0)

    def both(m, _):
        arrived(xb.at[m], fx, (m,))
        x = xb[m]
        hidden = matmul(x, up_n[...])
        scale = lax.rsqrt(jnp.sum(hidden * hidden, axis=1, keepdims=True) * (1.0 / feat) + EPS)
        v = hidden * scale * gain_row[...]
        v2 = v * v
        t = jnp.tanh(v * (C0 + (C0 * C1) * v2))
        half_v = 0.5 * v
        act[m] = (half_v + half_v * t).astype(BF16)
        slope = (0.5 + 0.5 * t) + half_v * (1.0 - t * t) * (C0 + (3.0 * C0 * C1) * v2)
        w = wh[0, m].astype(F32) * (slope * gain_row[...])
        mean = jnp.sum(w * hidden, axis=1, keepdims=True) * (1.0 / feat)
        d_hid = (scale * (w - hidden * (scale * scale * mean))).astype(BF16)
        mixed = matmul(d_hid, up_t[...].reshape(feat, width))
        gi[m] = (gb[m].astype(F32) + mixed).astype(BF16)
        copy(gi.at[m], gb.at[m], bg, (m,), (s - 1, r)).start()
        wh[0, m] = w.astype(BF16)
        wh[1, m] = hidden.astype(BF16)
        sc[m] = jnp.broadcast_to(scale, sc.shape[1:])
        x = x.astype(F32)
        xs[0, m] = (scale * x).astype(BF16)
        xs[1, m] = (x * (-(scale * scale * scale) * mean)).astype(BF16)
        return 0

    @pl.when(s == last)
    def _():
        def ahead(i, _):
            some = pl.ds(i * half, half)
            d_act = matmul(gb[some].reshape(half * ROWS, width), dn_n[...])
            wh[0, some] = d_act.astype(BF16).reshape(half, ROWS, feat)
            return 0

        def after(i, _):
            some = pl.ds(i * half, half)
            a = act[some].reshape(half * ROWS, feat)
            mixed = matmul(a, dn_t[...].reshape(feat, width)).reshape(half, ROWS, width)
            yb[some] = (xb[some].astype(F32) + mixed).astype(BF16)
            for j in range(half):
                m = i * half + j
                pltpu.make_async_copy(yb.at[m], codes_out.at[m], wr.at[m]).start()
            return 0

        lax.fori_loop(0, 2, ahead, 0)
        lax.fori_loop(0, micro, both, 0)
        lax.fori_loop(0, 2, after, 0)

    parts = (part_up, part_dn)
    rz, ry, z2, y2 = (rz_up, rz_dn), (ry_up, ry_dn), (rz2_up, rz2_dn), (ry2_up, ry2_dn)
    outs = (gu_out, gd_out)

    def part_y(a, e, h):
        return parts[a].at[2 * h:2 * h + 2, at_y(e), 0:CUT[a]]

    def part_z(a, d, g):
        return parts[a].at[d % NZ, 4 * g:4 * g + 4, CUT[a]:]

    def add_into(ref, other):
        ref[...] = (ref[...].astype(F32) + other[...].astype(F32)).astype(BF16)

    def ring_step(a, k, halves=(0, 1)):
        for h in halves:
            for side in range(2):
                steps = 4 if h == side else 3
                if k > steps:
                    continue
                ref = part_y(a, (steps - k, k - steps)[side], h)
                if k > 0:
                    got = rz[a].at[side, h, k - 1]
                    arrived(got, rz1, (a, side, h, k - 1))
                    add_into(ref, got)
                if k < steps:
                    send(ref, rz[a].at[side, h, k], rz1, (a, side, h, k), (right, left)[side])

    def line_send(a, side, d, g, cond):
        dst = ry[a].at[side, d - 1, 4 * g:4 * g + 4]
        send(part_z(a, (d, -d)[side], g), dst, ry1, (a, side, d - 1, g), (above, below)[side], cond)

    def line_step(a, d):
        for g in range(2):
            for side in range(2):
                way = (z, NZ - 1 - z)[side]
                got = ry[a].at[side, d, 4 * g:4 * g + 4]

                @pl.when((way >= 1) & (way <= NZ - 1 - d))
                def _():
                    arrived(got, ry1, (a, side, d, g))
                    add_into(part_z(a, (d, -d)[side], g), got)

                if d > 0:
                    line_send(a, side, d, g, way <= NZ - 1 - d)

    tokens = micro * ROWS

    def fill(a, h):
        for i in (2 * h, 2 * h + 1):
            cols = slice(group * i, group * (i + 1))
            if a == 1:
                left = act[:, :, cols].reshape(tokens, group)
                right = gb[...].reshape(tokens, width)
            else:
                left = wh[:, :, :, cols].reshape(2 * tokens, group)
                right = xs[...].reshape(2 * tokens, width)
            parts[a][i] = matmul(left, right, TN).astype(BF16).reshape(part_up.shape[1:])
        ring_step(a, 0, (h,))

    for a in (1, 0):
        fill(a, 0)
        fill(a, 1)
        for side in range(2):
            for g in range(2):
                line_send(a, side, NZ - 1, g, (z == 0, z == NZ - 1)[side])
    ring_step(1, 1)

    @pl.when(s > 0)
    def _():
        def gain_of(m, _):
            add_gain(m)
            return 0

        lax.fori_loop(0, micro, gain_of, 0)

    total = jnp.sum(gg_acc[...], axis=0, keepdims=True) / gain_row[...]
    gg_tot[...] = jnp.zeros_like(gg_tot)
    for d in range(NZ):
        for c in range(group // 128):
            lane = group * d + 128 * c
            gg_tot[0, pl.ds(at_z(d) * (group // 128) + c, 1), :] = total[:, lane:lane + 128]
    for d in range(1, NY):
        send(gg_tot.at[0], gg_y.at[d], hys, (d,), dev(z, at_y(d)))

    ring_step(0, 1)
    line_step(1, 2)
    line_step(0, 2)
    total = gg_tot[0]
    for d in range(1, NY):
        arrived(gg_y.at[d], hys, (d,))
        total = total + gg_y[d]
    gg_tot[1] = total
    for d in range(1, NZ):
        send(gg_tot.at[1], gg_z.at[d], hzs, (d,), dev(at_z(d), y))
    for k in (2, 3):
        for a in (1, 0):
            ring_step(a, k)
        for a in (1, 0):
            line_step(a, 3 - k)

    for a in (1, 0):
        for d in range(1, NY):
            send(parts[a].at[0, at_y(d), CUT[a]:], y2[a].at[d], ry2, (a, d), dev(z, at_y(d)))
    for a in (1, 0):
        kz = CUT[a]
        for h in range(2):
            ring_step(a, 4, (h,))
            for d in (2 * h, 2 * h + 1):
                if d > 0:
                    send(parts[a].at[d, y, 0:kz], z2[a].at[d], rz2, (a, d), dev(at_z(d), y))
    for a in (1, 0):
        kz = CUT[a]
        total = parts[a][0, y, kz:].astype(F32)
        for d in range(1, NY):
            arrived(y2[a].at[d], ry2, (a, d))
            total = total + y2[a][d].astype(F32)
        outs[a][kz:] = total
    for a in (1, 0):
        kz = CUT[a]
        total = parts[a][0, y, 0:kz].astype(F32)
        for d in range(1, NZ):
            arrived(z2[a].at[d], rz2, (a, d))
            total = total + z2[a][d].astype(F32)
        outs[a][0:kz] = total
    total = gg_tot[1]
    for d in range(1, NZ):
        arrived(gg_z.at[d], hzs, (d,))
        total = total + gg_z[d]
    gg_z[0] = total
    for i in range(8):
        head = min(piece, 128 - 16 * i)

        @pl.when(cut == i)
        def _():
            gg_out[:, 0:head] = gg_z[0, pl.ds(row, 1), 16 * i:16 * i + head]
            if head < piece:
                gg_out[:, head:] = gg_z[0, pl.ds(row + 1, 1), 0:piece - head]


    for c, cond in pending:
        if cond is None:
            c.wait_send()
        else:
            pl.when(cond)(c.wait_send)

    def drain(m, _):
        pltpu.make_async_copy(yb.at[m], codes_out.at[m], wr.at[m]).wait()

        @pl.when(s < last)
        def _():
            copy(yb.at[m], xb.at[m], fx, (m,), (s + 1, r)).wait_send()

        @pl.when(s > 0)
        def _():
            copy(gi.at[m], gb.at[m], bg, (m,), (s - 1, r)).wait_send()

        return 0

    lax.fori_loop(0, micro, drain, 0)


def hand_over(*refs):
    count = len(refs) // 2
    for i in range(count):
        refs[count + i][...] = refs[i][...]


def on_device(codes_in, cotangent, up, down, gain):
    rows, width = codes_in.shape
    piece = up.shape[2]
    feat = piece * lax.axis_size("replica")
    micro = rows // ROWS
    grid = (NZ, NY, piece, width)
    small = (-(-feat // 1024) * 8, 128)

    def vm(shape, dtype=BF16):
        return pltpu.VMEM(shape, dtype)

    def sem(*shape):
        return pltpu.SemaphoreType.DMA((2,) + shape)

    ku, kd = CUT
    scratch = [
        vm(grid), vm(grid), vm((width, feat)), vm((width, feat)), vm((1, feat), F32),
        vm((micro, ROWS, width)), vm((micro, ROWS, width)), vm((micro, ROWS, width)),
        vm((micro, ROWS, feat)), vm((2, micro, ROWS, feat)), vm((micro, ROWS, feat)),
        vm((2, micro, ROWS, width)), vm((micro, ROWS, 128), F32),
        vm((micro, ROWS, width), F32), vm((micro, ROWS, width), F32),
        vm(grid), vm(grid),
        vm((2, 2, 4, 2, ku, width)), vm((2, 2, 4, 2, kd, width)),
        vm((2, NZ, NY, piece - ku, width)), vm((2, NZ, NY, piece - kd, width)),
        vm((NZ, ku, width)), vm((NZ, kd, width)),
        vm((NY, piece - ku, width)), vm((NY, piece - kd, width)),
        vm(small, F32), vm(small, F32), vm((NY,) + small, F32), vm((NZ,) + small, F32),
        vm((8, feat), F32), vm((2,) + small, F32), vm((NY,) + small, F32), vm((NZ,) + small, F32),
        sem(2, NZ), sem(2, 2, 4), sem(2, 2, 2, 4), sem(2, 2, 3), sem(NY), sem(NZ),
        sem(micro), sem(micro),
        sem(2, 2, 2, 4), sem(2, 2, NZ, 2), sem(2, NZ), sem(2, NY), sem(NY), sem(NZ),
        vm((micro, ROWS, width)), pltpu.SemaphoreType.DMA((2,)), pltpu.SemaphoreType.DMA((micro,)),
    ]
    results = pl.pallas_call(
        kernel,
        out_shape=(
            jax.ShapeDtypeStruct((micro, ROWS, width), BF16),
            jax.ShapeDtypeStruct((piece, width), F32),
            jax.ShapeDtypeStruct((piece, width), F32),
            jax.ShapeDtypeStruct((1, piece), F32),
        ),
        in_specs=[pl.BlockSpec(memory_space=pl.ANY)] * 2 + [pl.BlockSpec(memory_space=pltpu.VMEM)] * 3,
        out_specs=(pl.BlockSpec(memory_space=pl.ANY),) + (pl.BlockSpec(memory_space=pltpu.VMEM),) * 3,
        scratch_shapes=scratch,
        compiler_params=pltpu.CompilerParams(
            collective_id=0, has_side_effects=True, vmem_limit_bytes=56 << 20
        ),
    )(codes_in.reshape(micro, ROWS, width), cotangent.reshape(micro, ROWS, width), up[0].T, down[0].T, gain)
    codes, grad_up, grad_dn, grad_gain = pl.pallas_call(
        hand_over,
        out_shape=tuple(jax.ShapeDtypeStruct(x.shape, x.dtype) for x in results),
        in_specs=[pl.BlockSpec(memory_space=pltpu.VMEM)] * len(results),
        out_specs=tuple([pl.BlockSpec(memory_space=pltpu.VMEM)] * len(results)),
    )(*results)
    return (codes.reshape(1, rows, width), grad_up.T[None], grad_dn.T[None], grad_gain)


def solution(mesh):
    placed = (
        P("replica", None),
        P("replica", None),
        P("section", None, "replica"),
        P("section", None, "replica"),
        P("section", "replica"),
    )
    return jax.shard_map(
        on_device,
        mesh=mesh,
        in_specs=placed,
        out_specs=(
            P("section", "replica", None),
            P("section", None, "replica"),
            P("section", None, "replica"),
            P("section", "replica"),
        ),
        check_vma=False,
    )
```
